128 devices in a mesh: comp: 2 (over z_lo), tx: 8 (over z_hi, x), ty: 8 (over y, core).
Axes of the slice: x: 4, y: 4, z: 4 (z_hi: 2, z_lo: 2; z = z_hi * 2 + z_lo), core: 2. Of those that a mesh axis runs over, the one named last changes fastest.
Arguments:
- state: float32 [2, 16, 1024, 4096], P('comp', None, 'tx', 'ty'), may hold values from -6 to 6
- coefs: float32 [2, 3, 1024, 4096], P('comp', None, 'tx', 'ty'), may hold values from -0.2 to 0.2
- land_sea: int32 [1024, 4096], P('tx', 'ty'), may hold values 0 or 1
- gamma: float32 [2, 8], P('comp'), may hold values from 0.1 to 0.4
- pair_src: int32 [2, 32768], P('comp', ('tx', 'ty')), may hold values from 0 to 511
- pair_dev: int32 [2, 32768, 1], P('comp', ('tx', 'ty')), may hold values from 0 to 63; in each aligned block of 512 rows (0 to 511, 512 to 1023, ..., all dimensions but the last counted through in order) at most 16 rows name the same one
- pair_blk: int32 [2, 32768], P('comp', ('tx', 'ty')), may hold values from 0 to 511
- weights: bfloat16 [2, 32768, 128, 128], P('comp', ('tx', 'ty')), may hold values from -0.375 to 0.375
Outputs:
- new_state: float32 [2, 16, 1024, 4096], P('comp', None, 'tx', 'ty')
- remapped: float32 [2, 8, 1024, 4096], P('comp', None, 'tx', 'ty')
The draws below stay inside these ranges and needn't reach their ends.
Inputs may be any that keep to these rules, and one draw needn't show every extreme that they name: `pair_dev`: among the 512 weight blocks of one tile of one component, at most 16 name the same target tile, a bound that some block reaches.
All inputs are finite; a program needn't handle non-finite values. No bound on the sum of `land_sea` on one device may be relied on, other than what follows from the above.
Results may differ from the reference program's by a relative error of at most 0.0029.
Values sent between devices are 32-bit elements; how exact they have to be, the bound alone decides.
A program may use at most 128 MiB of HBM per device.

```python
import math
import jax
import jax.numpy as jnp
import numpy as np
from jax import lax

NF = 16
CH = 8
BLK = 128
CX = 128
CY = 512
PAIRS = 512
TILES = 64
NB = 512
CAP = 16
NX = 1024
NY = 4096
N_TX = 8
N_TY = 8


def with_ends(entries, own_key, low, high):
    index_at = [jax.random.randint(jax.random.fold_in(own_key, axis), (), 0, length) for axis, length in enumerate(entries.shape)]
    widest = entries.shape.index(max(entries.shape))
    neighbour = index_at[:widest] + [(index_at[widest] + 1) % entries.shape[widest]] + index_at[widest + 1:]
    return entries.at[tuple(index_at)].set(low).at[tuple(neighbour)].set(high)


def block_scale(rng, dims, shards, low, largest):
    def one(dim, shards_of):
        draws = jax.random.uniform(jax.random.fold_in(jax.random.fold_in(rng, 6), dim), (shards_of,), jnp.float32, low / len(shards), largest / len(shards))
        return jnp.repeat(jnp.exp(draws), dims[dim] // shards_of).reshape((-1,) + (1,) * (len(dims) - dim - 1))

    factor_of = one(*shards[0])
    for cut in shards[1:]:
        factor_of = factor_of * one(*cut)
    return factor_of


def deal_out(stream_key, own, number, rows, number_of, top, reach, skew):
    order = jax.random.permutation(stream_key, number_of)
    crowded, common = shares(number_of, rows * top, reach, skew, True), shares(number_of, rows * top, reach, skew, False)
    places = jnp.arange(number_of)

    def named(tallies, offset_by):
        used = int((tallies > 0).sum())
        fixed = max(1, used // 4)
        moved = fixed + (places - fixed + offset_by * (used - fixed)) % max(1, number_of - fixed)
        return jnp.zeros((number_of,), jnp.int32).at[order[jnp.where(places < fixed, places, moved)]].set(jnp.asarray(tallies, jnp.int32))

    tallies = jnp.where(number % 4 == 0, named(crowded, number // 4), named(common, number - number // 4 - 1))
    mixed = jax.random.permutation(jax.random.fold_in(own, 3), number_of)
    source_of, taker = mixed[0:number_of // 2 * 2:2], mixed[1:number_of // 2 * 2:2]
    margin = jnp.minimum(tallies[source_of] - 1, reach - tallies[taker]) // 2
    margin = jnp.where((source_of == order[0]) | (taker == order[0]) | (tallies[taker] == 0), 0, jnp.maximum(margin, 0))
    moved = jax.random.randint(jax.random.fold_in(own, 4), (number_of // 2,), 0, 1 << 20) % (margin + 1)
    tallies = tallies.at[source_of].add(-moved).at[taker].add(moved)
    items = jnp.searchsorted(jnp.cumsum(tallies), jnp.arange(rows * top), side="right").astype(jnp.int32)
    table = items.reshape(top, rows).T
    table = table[jax.random.permutation(jax.random.fold_in(own, 1), rows)]
    offset_by = jax.random.randint(jax.random.fold_in(own, 2), (rows, 1), 0, top)
    return jnp.take_along_axis(table, (jnp.arange(top)[None, :] + offset_by) % top, axis=1)


def shares(count, total, reach, slope, full):
    portions = [(1 << 20) // math.isqrt(rank ** slope) + 1 for rank in range(1, count + 1)]
    largest = reach if full else min(reach, max(-(-total // count), total * portions[0] // sum(portions)))
    least = 1 if total - largest >= count - 1 else 0
    given, rest = [largest] + [least] * (count - 1), total - largest - least * (count - 1)
    while rest > 0:
        candidates = [i for i in range(1, count) if given[i] < largest] or [i for i in range(1, count) if given[i] < reach]
        mass, budget = sum([portions[i] for i in candidates]), rest
        for i in candidates:
            addition = min(reach - given[i], max(1, budget * portions[i] // mass), rest)
            given[i] = given[i] + addition
            rest = rest - addition
    return np.array(given)


def noise(own_key, shape, spread, most, cuts=(), held_as=jnp.bfloat16):
    array = jax.random.normal(own_key, shape, jnp.float32) * spread
    if len(cuts) > 0:
        array = block_scale(own_key, shape, cuts, -0.22, 0.18) * array
    return jnp.clip(array, min=-most, max=most).astype(held_as)


def setup_inputs(seed: int = 0) -> dict:
    key_of = jax.random.split(jax.random.key(seed), 9)
    state = noise(key_of[0], (2, NF, NX, NY), 1.0, 6.0, ((0, 2), (2, 8), (3, 8)), jnp.float32)
    coefs = jnp.clip(jax.random.uniform(key_of[1], (2, 3, NX, NY), jnp.float32, -0.2, 0.2) * block_scale(key_of[1], (2, 3, NX, NY), ((0, 2), (2, 8), (3, 8)), -0.4, 0.0), -0.2, 0.2)
    land_sea = with_ends((jax.random.randint(key_of[2], (NX, NY), 0, 10) < 7).astype(jnp.int32), jax.random.fold_in(key_of[2], 1), 0, 1)
    gamma = jnp.clip(jnp.exp(math.log(0.4) - 1.3862944 * jax.random.uniform(key_of[3], (2, CH), jnp.float32) ** block_scale(key_of[3], (2, CH), ((0, 2),), -0.2, 0.2)), 0.1, 0.4)
    pair_src = with_ends(jax.random.randint(key_of[4], (2, TILES * PAIRS), 0, NB), jax.random.fold_in(key_of[4], 1), 0, NB - 1).astype(jnp.int32)
    pair_dev_keys = jax.random.split(jax.random.fold_in(key_of[5], 1), 2 * (TILES * PAIRS) // PAIRS)
    pair_dev_turns = jax.random.permutation(jax.random.fold_in(key_of[5], 3), 2 * (TILES * PAIRS) // PAIRS)
    pair_dev = jax.vmap(lambda own, number: deal_out(jax.random.fold_in(key_of[5], 2), own, number, PAIRS, TILES, 1, CAP, 2))(pair_dev_keys, pair_dev_turns).reshape((2, TILES * PAIRS, 1))
    pair_blk = with_ends(jax.random.randint(key_of[6], (2, TILES * PAIRS), 0, NB), jax.random.fold_in(key_of[6], 1), 0, NB - 1).astype(jnp.int32)
    weights = noise(key_of[7], (2, TILES * PAIRS, BLK, BLK), (2 * BLK) ** -0.5, 0.375, ((0, 2), (1, 64)))
    return dict(state=state, coefs=coefs, land_sea=land_sea, gamma=gamma, pair_src=pair_src, pair_dev=pair_dev, pair_blk=pair_blk, weights=weights)


def tendency(padded, coefs, recv, gamma, keep):
    center = padded[:, 1:-1, 1:-1]
    xminus = padded[:, :-2, 1:-1]
    xplus = padded[:, 2:, 1:-1]
    yminus = padded[:, 1:-1, :-2]
    yplus = padded[:, 1:-1, 2:]
    speed_x = coefs[0]
    speed_y = coefs[1]
    kappa = coefs[2]
    advect = -(jnp.maximum(speed_x, 0.0) * (center - xminus) + jnp.minimum(speed_x, 0.0) * (xplus - center))
    advect = advect - (jnp.maximum(speed_y, 0.0) * (center - yminus) + jnp.minimum(speed_y, 0.0) * (yplus - center))
    diffuse = kappa * (xplus + xminus + yplus + yminus - 4.0 * center)
    chan = recv.shape[0]
    couple = gamma[:, None, None] * (recv - center[:chan])
    couple = jnp.concatenate([couple, jnp.zeros_like(center[chan:])], axis=0)
    return keep * (advect + diffuse + couple)


def to_blocks(field):
    two, chan = field.shape[0], field.shape[1]
    tiled = field.reshape(two, chan, N_TX, CX, N_TY, CY).transpose(0, 1, 2, 4, 3, 5)
    return tiled.reshape(two, chan, N_TX * N_TY * (CX * CY // BLK), BLK)


def from_blocks(blocks):
    two, chan = blocks.shape[0], blocks.shape[1]
    tiled = blocks.reshape(two, chan, N_TX, N_TY, CX, CY).transpose(0, 1, 2, 4, 3, 5)
    return tiled.reshape(two, chan, N_TX * CX, N_TY * CY)


def reference(state, coefs, land_sea, gamma, pair_src, pair_dev, pair_blk, weights):
    tiles = N_TX * N_TY
    nblock = CX * CY // BLK
    surface = to_blocks(state[:, :CH]).astype(jnp.bfloat16)
    owner = jnp.arange(tiles * PAIRS, dtype=jnp.int32) // PAIRS
    received = []
    for comp in range(2):
        source = (owner * nblock + pair_src[comp]).astype(jnp.int32)
        picked = jnp.take(surface[comp], source, axis=1)
        picked = picked.transpose(1, 0, 2).reshape(tiles, PAIRS, CH, BLK)
        blocks = weights[comp].reshape(tiles, PAIRS, BLK, BLK)

        def apply_tile(pieces):
            return jnp.einsum("pts,pcs->pct", pieces[0].astype(jnp.float32), pieces[1].astype(jnp.float32))

        contrib = lax.map(apply_tile, (blocks, picked)).reshape(tiles * PAIRS, CH, BLK)
        target = (pair_dev[comp, :, 0] * nblock + pair_blk[comp]).astype(jnp.int32)
        summed = jax.ops.segment_sum(contrib, target, num_segments=tiles * nblock)
        received.append(summed.transpose(1, 0, 2))
    remapped = from_blocks(jnp.stack([received[1], received[0]]))
    results = []
    for comp in range(2):
        if comp == 0:
            keep = jnp.ones(land_sea.shape, jnp.float32)
            mix_a, mix_b = 0.0, 1.0
        else:
            keep = land_sea.astype(jnp.float32)
            mix_a, mix_b = 0.5, 0.5
        start = state[comp]
        first = tendency(jnp.pad(start, ((0, 0), (1, 1), (1, 1))), coefs[comp], remapped[comp], gamma[comp], keep)
        section = start + first
        second = tendency(jnp.pad(section, ((0, 0), (1, 1), (1, 1))), coefs[comp], remapped[comp], gamma[comp], keep)
        results.append(mix_a * start + (1.0 - mix_a) * section + mix_b * second)
    return jnp.stack(results), remapped
```

```python
import jax
import jax.numpy as jnp
from jax import lax
from jax.experimental import pallas as pl
from jax.experimental.pallas import tpu as pltpu
from jax.sharding import PartitionSpec as P

MESH = pl.DeviceIdType.MESH
F32 = jnp.float32
BF16 = jnp.bfloat16


def extended(cells, sides, width):
    for axis, dim in sides:
        count = lax.axis_size(axis)
        ends = count - 1
        head = lax.slice_in_dim(cells, 0, width, axis=dim)
        tail = lax.slice_in_dim(cells, cells.shape[dim] - width, cells.shape[dim], axis=dim)
        cells = jnp.concatenate(
            [
                lax.ppermute(tail, axis, [(i, (i + 1) % count) for i in range(ends)]),
                cells,
                lax.ppermute(head, axis, [((i + 1) % count, i) for i in range(ends)]),
            ],
            axis=dim,
        )
    return cells


def tendency(padded, coefs, recv, gamma, keep):
    center = padded[:, 1:-1, 1:-1]
    xminus = padded[:, :-2, 1:-1]
    xplus = padded[:, 2:, 1:-1]
    yminus = padded[:, 1:-1, :-2]
    yplus = padded[:, 1:-1, 2:]
    speed_x = coefs[0]
    speed_y = coefs[1]
    kappa = coefs[2]
    advect = -(
        jnp.maximum(speed_x, 0.0) * (center - xminus) + jnp.minimum(speed_x, 0.0) * (xplus - center)
    )
    advect = advect - (
        jnp.maximum(speed_y, 0.0) * (center - yminus) + jnp.minimum(speed_y, 0.0) * (yplus - center)
    )
    diffuse = kappa * (xplus + xminus + yplus + yminus - 4.0 * center)
    chan = recv.shape[0]
    couple = gamma[:, None, None] * (recv - center[:chan])
    couple = jnp.concatenate([couple, jnp.zeros_like(center[chan:])], axis=0)
    return keep * (advect + diffuse + couple)


def shallow_rims(field):
    return extended(field, (("tx", 1), ("ty", 2)), 1)


TILES = 64
PAIRS = 512
CAP = 16
SLOTS = TILES * CAP
NB = 512
CH = 8


def plan_kernel(src, dev, blk, slot_k, slot_src, slot_id, count):
    def clear(i, carry):
        slot_k[i] = 0
        slot_src[i] = 0
        slot_id[i] = NB
        return carry

    lax.fori_loop(0, SLOTS, clear, 0, unroll=8)

    def clear_count(i, carry):
        count[i] = 0
        return carry

    lax.fori_loop(0, TILES, clear_count, 0, unroll=8)

    def place(k, carry):
        d = dev[k]
        r = count[d]
        count[d] = r + 1
        s = d * CAP + r
        b = blk[k]
        x = b >> 2
        slot_k[s] = k
        slot_src[s] = src[k]
        slot_id[s] = (x >> 3) * 32 + (b & 3) * 8 + (x & 7)
        return carry

    lax.fori_loop(0, PAIRS, place, 0, unroll=8)


def plan(src, dev, blk):
    smem = pl.BlockSpec(memory_space=pltpu.SMEM)
    return pl.pallas_call(
        plan_kernel,
        out_shape=[jax.ShapeDtypeStruct((SLOTS,), jnp.int32)] * 3,
        in_specs=[smem] * 3,
        out_specs=[smem] * 3,
        scratch_shapes=[pltpu.SMEM((TILES,), jnp.int32)],
    )(src, dev, blk)


def remap_kernel(
    slot_k,
    slot_src,
    ids,
    state,
    weights,
    out,
    wbuf,
    surf,
    send,
    recv,
    recv_ids,
    acc,
    wsem,
    ssem,
    rsem,
    isend,
    irecv,
):
    comp = lax.axis_index("comp")
    tx = lax.axis_index("tx")
    ty = lax.axis_index("ty")
    h = tx // 4
    x = tx % 4
    y = ty // 2
    core = ty % 2
    sign = 1 - 2 * core

    load = pltpu.make_async_copy(weights.at[0], wbuf, wsem)
    load.start()

    def partner(i):
        dh = lax.rem(i, 2)
        dx = lax.rem(lax.div(i, 2), 4)
        dy = lax.rem(lax.div(i, 8) + dx, 4)
        dc = lax.div(i, 32)
        to_x = lax.rem(h + dh, 2) * 4 + lax.rem(x + sign * dx + 4, 4)
        to_y = lax.rem(y + sign * dy + 4, 4) * 2 + lax.rem(core + dc, 2)
        return to_x, to_y

    barrier = pltpu.get_barrier_semaphore()

    def greet(i, carry):
        to_x, to_y = partner(i)
        pl.semaphore_signal(barrier, 1, device_id=(1 - comp, to_x, to_y), device_id_type=MESH)
        return carry

    lax.fori_loop(0, TILES, greet, 0)

    def relay(i, carry):
        for yb in range(4):
            rows = pl.ds(pl.multiple_of(i * 8, 8), 8)
            tiles = state[0, :, rows, yb * 128 : yb * 128 + 128]
            tiles = jnp.swapaxes(tiles, 0, 1)
            for r in range(8):
                surf[i * 32 + r * 4 + yb] = tiles[r]
        return carry

    lax.fori_loop(0, 16, relay, 0)
    pl.semaphore_wait(barrier, TILES)

    def copies(i):
        to_x, to_y = partner(i)
        to = (1 - comp, to_x, to_y)
        data = pltpu.make_async_remote_copy(
            send.at[i], recv.at[i], ssem.at[i], rsem.at[i], device_id=to, device_id_type=MESH
        )
        names = pltpu.make_async_remote_copy(
            ids.at[to_x * 8 + to_y],
            recv_ids.at[i],
            isend.at[i],
            irecv.at[i],
            device_id=to,
            device_id_type=MESH,
        )
        return data, names, to_x * 8 + to_y

    load.wait()

    def produce(i, carry):
        data, names, tile = copies(i)
        names.start()
        zero = jnp.zeros((8, 128), F32)
        for g in range(CAP // 4):
            ws = []
            ps = []
            for j in range(4):
                s = tile * CAP + g * 4 + j
                ws.append(wbuf[slot_k[s]])
                ps.append(surf[slot_src[s]])
            lhs = jnp.concatenate(
                [
                    jnp.concatenate([ps[0], zero, ps[2], zero], axis=0),
                    jnp.concatenate([zero, ps[1], zero, ps[3]], axis=0),
                ],
                axis=1,
            ).astype(BF16)
            rhs = jnp.concatenate(
                [
                    jnp.concatenate([ws[0], ws[1]], axis=1),
                    jnp.concatenate([ws[2], ws[3]], axis=1),
                ],
                axis=0,
            )
            both = lax.dot_general(
                lhs, rhs, (((1,), (1,)), ((), ())), preferred_element_type=F32
            )
            parts = [both[0:8, :128], both[8:16, :128], both[16:24, 128:], both[24:32, 128:]]
            for j in range(4):
                send[i, pl.ds(g * 4 + j, 8, stride=CAP), :] = parts[j]
        data.start()
        return carry

    lax.fori_loop(0, TILES, produce, 0)

    def arrive(i, carry):
        data, names, _ = copies(i)
        names.wait_recv()
        data.wait_recv()
        return carry

    seg = lax.broadcasted_iota(jnp.int32, (8, 128), 1) // CAP == lax.broadcasted_iota(
        jnp.int32, (8, 128), 0
    )
    for q in range(4):
        lax.fori_loop(16 * q, 16 * q + 16, arrive, 0)
        lanes = []
        for half in range(2):
            first = q * 16 + half * 8
            rows = jnp.concatenate([recv_ids[first + j] for j in range(8)], axis=0)
            lanes.append(jnp.sum(jnp.where(seg, rows, 0.0), axis=0, keepdims=True))
        wanted = jnp.concatenate(lanes, axis=1)
        blocks = lax.broadcasted_iota(jnp.int32, (NB, 256), 0).astype(F32)
        select = jnp.where(blocks == wanted, 1.0, 0.0).astype(BF16)
        for c in range(0, CH, 2):
            cols = []
            for cc in (c, c + 1):
                cols.append(
                    jnp.concatenate(
                        [recv[q * 16 + j, cc * CAP : cc * CAP + CAP, :] for j in range(16)], axis=0
                    )
                )
            terms = jnp.concatenate(cols, axis=1)
            high = terms.astype(BF16)
            low = (terms - high.astype(F32)).astype(BF16)
            total = jnp.dot(select, high, preferred_element_type=F32)
            total = total + jnp.dot(select, low, preferred_element_type=F32)
            for cc in range(2):
                piece = total[:, cc * 128 : cc * 128 + 128]
                if q == 0:
                    acc[c + cc] = piece
                else:
                    acc[c + cc] += piece

    def unfold(i, carry):
        for yb in range(4):
            for c in range(CH):
                out[c, pl.ds(pl.multiple_of(i * 8, 8), 8), yb * 128 : yb * 128 + 128] = acc[
                    c, pl.ds(pl.multiple_of(i * 32 + yb * 8, 8), 8), :
                ]
        return carry

    lax.fori_loop(0, 16, unfold, 0)

    def sent(i, carry):
        data, names, _ = copies(i)
        names.wait_send()
        data.wait_send()
        return carry

    lax.fori_loop(0, TILES, sent, 0)


def remap(slot_k, slot_src, ids, state, weights):
    smem = pl.BlockSpec(memory_space=pltpu.SMEM)
    vmem = pl.BlockSpec(memory_space=pltpu.VMEM)
    return pl.pallas_call(
        remap_kernel,
        grid=(1,),
        out_shape=jax.ShapeDtypeStruct((CH, 128, 512), F32),
        in_specs=[
            smem,
            smem,
            vmem,
            pl.BlockSpec((1, CH, 128, 512), lambda g: (0, 0, 0, 0)),
            pl.BlockSpec(memory_space=pl.ANY),
        ],
        out_specs=vmem,
        scratch_shapes=[
            pltpu.VMEM((PAIRS, 128, 128), BF16),
            pltpu.VMEM((NB, CH, 128), F32),
            pltpu.VMEM((TILES, CH * CAP, 128), F32),
            pltpu.VMEM((TILES, CH * CAP, 128), F32),
            pltpu.VMEM((TILES, 1, 128), F32),
            pltpu.VMEM((CH, NB, 128), F32),
            pltpu.SemaphoreType.DMA,
            pltpu.SemaphoreType.DMA((TILES,)),
            pltpu.SemaphoreType.DMA((TILES,)),
            pltpu.SemaphoreType.DMA((TILES,)),
            pltpu.SemaphoreType.DMA((TILES,)),
        ],
        compiler_params=pltpu.CompilerParams(
            collective_id=0, has_side_effects=True, vmem_limit_bytes=56 << 20
        ),
    )(slot_k, slot_src, ids, state, weights)


def body(state, coefs, land_sea, gamma, pair_src, pair_dev, pair_blk, weights):
    comp_index = lax.axis_index("comp")
    cells_x, cells_y = state.shape[2], state.shape[3]
    slot_k, slot_src, slot_id = plan(
        pair_src.reshape(PAIRS), pair_dev.reshape(PAIRS), pair_blk.reshape(PAIRS)
    )
    ids = jnp.tile(slot_id.astype(F32).reshape(TILES, 1, CAP), (1, 1, 8))
    recv = remap(slot_k, slot_src, ids, state, weights)
    is_atmos = comp_index == 0
    keep = jnp.where(
        is_atmos, jnp.ones((cells_x, cells_y), jnp.float32), land_sea.astype(jnp.float32)
    )
    mix_a = jnp.where(is_atmos, 0.0, 0.5).astype(jnp.float32)
    mix_b = jnp.where(is_atmos, 1.0, 0.5).astype(jnp.float32)
    start = state[0]
    local_coefs = coefs[0]
    rates = gamma[0]
    first = tendency(shallow_rims(start), local_coefs, recv, rates, keep)
    section = start + first
    second = tendency(shallow_rims(section), local_coefs, recv, rates, keep)
    result = mix_a * start + (1.0 - mix_a) * section + mix_b * second
    return (result[None], recv[None])


def solution(mesh):
    placed = (
        P("comp", None, "tx", "ty"),
        P("comp", None, "tx", "ty"),
        P("tx", "ty"),
        P("comp", None),
        P("comp", ("tx", "ty")),
        P("comp", ("tx", "ty"), None),
        P("comp", ("tx", "ty")),
        P("comp", ("tx", "ty"), None, None),
    )
    return jax.shard_map(
        body,
        mesh=mesh,
        in_specs=placed,
        out_specs=(P("comp", None, "tx", "ty"), P("comp", None, "tx", "ty")),
        check_vma=False,
    )
```

```python
import jax
import jax.numpy as jnp
from jax import lax
from jax.experimental import pallas as pl
from jax.experimental.pallas import tpu as pltpu
from jax.sharding import PartitionSpec as P

MESH = pl.DeviceIdType.MESH
F32 = jnp.float32
BF16 = jnp.bfloat16


TILES = 64
PAIRS = 512
CAP = 16
SLOTS = TILES * CAP
NB = 512
CH = 8
NF = 16
CX = 128
CY = 512


def plan_kernel(src, dev, blk, slot_k, slot_src, slot_id, count):
    def clear(i, carry):
        slot_k[i] = 0
        slot_src[i] = 0
        slot_id[i] = NB
        return carry

    lax.fori_loop(0, SLOTS, clear, 0, unroll=8)

    def clear_count(i, carry):
        count[i] = 0
        return carry

    lax.fori_loop(0, TILES, clear_count, 0, unroll=8)

    def place(k, carry):
        d = dev[k]
        r = count[d]
        count[d] = r + 1
        s = d * CAP + r
        b = blk[k]
        x = b >> 2
        slot_k[s] = k
        slot_src[s] = src[k]
        slot_id[s] = (x >> 3) * 32 + (b & 3) * 8 + (x & 7)
        return carry

    lax.fori_loop(0, PAIRS, place, 0, unroll=8)


def plan(src, dev, blk):
    smem = pl.BlockSpec(memory_space=pltpu.SMEM)
    return pl.pallas_call(
        plan_kernel,
        out_shape=[jax.ShapeDtypeStruct((SLOTS,), jnp.int32)] * 3,
        in_specs=[smem] * 3,
        out_specs=[smem] * 3,
        scratch_shapes=[pltpu.SMEM((TILES,), jnp.int32)],
    )(src, dev, blk)


def slopes(i, coefs, land, comp, kc):
    rows = pl.ds(pl.multiple_of(i * 8, 8), 8)
    u = coefs[0, 0, rows, :]
    v = coefs[0, 1, rows, :]
    kappa = coefs[0, 2, rows, :]
    keep = jnp.where(comp == 0, 1.0, land[rows, :].astype(F32))
    kc[0, rows, :] = keep * (jnp.maximum(u, 0.0) + kappa)
    kc[1, rows, :] = keep * (kappa - jnp.minimum(u, 0.0))
    kc[2, rows, :] = keep * (jnp.maximum(v, 0.0) + kappa)
    kc[3, rows, :] = keep * (kappa - jnp.minimum(v, 0.0))
    kc[4, rows, :] = -keep * (jnp.abs(u) + jnp.abs(v) + 4.0 * kappa)
    kc[5, rows, :] = keep


def stencil(cur, prev, nxt, left, right, weight):
    sub = lax.broadcasted_iota(jnp.int32, (8, CY), 0)
    lane = lax.broadcasted_iota(jnp.int32, (8, CY), 1)
    up = jnp.where(sub == 0, pltpu.roll(prev, 1, 0), pltpu.roll(cur, 1, 0))
    down = jnp.where(sub == 7, pltpu.roll(nxt, 7, 0), pltpu.roll(cur, 7, 0))
    back = jnp.where(lane == 0, left, pltpu.roll(cur, 1, 1))
    ahead = jnp.where(lane == CY - 1, right, pltpu.roll(cur, CY - 1, 1))
    total = weight[0] * up + weight[1] * down
    total = total + (weight[2] * back + weight[3] * ahead)
    return total + weight[4] * cur


def mixes(comp):
    a = jnp.where(comp == 0, 0.0, 0.5).astype(F32)
    b = jnp.where(comp == 0, 1.0, 0.5).astype(F32)
    return a, b


def remap_kernel(
    slot_k,
    slot_src,
    gamma,
    ids,
    coefs,
    land,
    state,
    weights,
    out,
    section,
    rest,
    halo_x,
    halo_y,
    wbuf,
    surf,
    send,
    recv,
    recv_ids,
    acc,
    sp,
    sq,
    part,
    kc,
    xs,
    xr,
    ys,
    yr,
    lsem,
    ssem,
    rsem,
    isend,
    irecv,
    esend,
    erecv,
):
    comp = lax.axis_index("comp")
    tx = lax.axis_index("tx")
    ty = lax.axis_index("ty")
    h = tx // 4
    x = tx % 4
    y = ty // 2
    core = ty % 2
    sign = 1 - 2 * core

    load_state = pltpu.make_async_copy(state.at[0], sp.at[:, 8 : 8 + CX, :], lsem.at[0])
    load_state.start()
    load = pltpu.make_async_copy(weights.at[0], wbuf, lsem.at[1])
    load.start()

    def partner(i):
        dh = lax.rem(i, 2)
        dx = lax.rem(lax.div(i, 2), 4)
        dy = lax.rem(lax.div(i, 8) + dx, 4)
        dc = lax.div(i, 32)
        to_x = lax.rem(h + dh, 2) * 4 + lax.rem(x + sign * dx + 4, 4)
        to_y = lax.rem(y + sign * dy + 4, 4) * 2 + lax.rem(core + dc, 2)
        return to_x, to_y

    beside = (
        (comp, lax.rem(tx + 1, 8), ty),
        (comp, lax.rem(tx + 7, 8), ty),
        (comp, tx, lax.rem(ty + 1, 8)),
        (comp, tx, lax.rem(ty + 7, 8)),
    )

    barrier = pltpu.get_barrier_semaphore()

    def greet(i, carry):
        to_x, to_y = partner(i)
        pl.semaphore_signal(barrier, 1, device_id=(1 - comp, to_x, to_y), device_id_type=MESH)
        return carry

    lax.fori_loop(0, TILES, greet, 0)
    for to in beside:
        pl.semaphore_signal(barrier, 1, device_id=to, device_id_type=MESH)

    def prepare(i, carry):
        slopes(i, coefs, land, comp, kc)
        return carry

    lax.fori_loop(0, 16, prepare, 0)
    load_state.wait()

    def relay(i, carry):
        for yb in range(4):
            rows = pl.ds(pl.multiple_of(i * 8 + 8, 8), 8)
            tiles = sp[0:CH, rows, yb * 128 : yb * 128 + 128]
            tiles = jnp.swapaxes(tiles, 0, 1)
            for r in range(8):
                surf[i * 32 + r * 4 + yb] = tiles[r]
        return carry

    lax.fori_loop(0, 16, relay, 0)

    def edges(e):
        moves = []
        for n in range(4):
            count = NF if e == 0 else CH
            if n < 2:
                box = (xs.at[e, n, 0:count], xr.at[e, n, 0:count])
            else:
                box = (ys.at[e, n - 2], yr.at[e, n - 2])
            moves.append(
                pltpu.make_async_remote_copy(
                    box[0],
                    box[1],
                    esend.at[e, n],
                    erecv.at[e, n],
                    device_id=beside[n],
                    device_id_type=MESH,
                )
            )
        return moves

    lanes = lax.broadcasted_iota(jnp.int32, (8, 128), 1)

    def pack_columns(e, i, strips):
        first = jnp.zeros((8, 128), F32)
        last = jnp.zeros((8, 128), F32)
        for f, cells in enumerate(strips):
            first = jnp.where(lanes == f, cells[:, 0:1], first)
            last = jnp.where(lanes == f, cells[:, -1:], last)
        rows = pl.ds(pl.multiple_of(i * 8, 8), 8)
        ys[e, 0, rows, :] = last
        ys[e, 1, rows, :] = first

    def settle(e):
        for move in edges(e):
            move.wait_recv()
        for n, (place, end) in enumerate(((tx, 0), (tx, 7))):
            count = NF if e == 0 else CH
            xr[e, n, 0:count] = jnp.where(place == end, 0.0, xr[e, n, 0:count])
        for n, (place, end) in enumerate(((ty, 0), (ty, 7))):
            yr[e, n] = jnp.where(place == end, 0.0, yr[e, n])

    def pack_state(i, carry):
        rows = pl.ds(pl.multiple_of(i * 8 + 8, 8), 8)
        pack_columns(0, i, [sp[f, rows, :] for f in range(NF)])
        return carry

    lax.fori_loop(0, 16, pack_state, 0)
    for f in range(NF):
        xs[0, 0, f : f + 1, :] = sp[f, 7 + CX : 8 + CX, :]
        xs[0, 1, f : f + 1, :] = sp[f, 8:9, :]

    pl.semaphore_wait(barrier, TILES + 4)
    for move in edges(0):
        move.start()

    def copies(i):
        to_x, to_y = partner(i)
        to = (1 - comp, to_x, to_y)
        data = pltpu.make_async_remote_copy(
            send.at[i], recv.at[i], ssem.at[i], rsem.at[i], device_id=to, device_id_type=MESH
        )
        names = pltpu.make_async_remote_copy(
            ids.at[to_x * 8 + to_y],
            recv_ids.at[i],
            isend.at[i],
            irecv.at[i],
            device_id=to,
            device_id_type=MESH,
        )
        return data, names, to_x * 8 + to_y

    load.wait()

    def produce(i, carry):
        data, names, tile = copies(i)
        names.start()
        zero = jnp.zeros((8, 128), F32)
        for g in range(CAP // 4):
            ws = []
            ps = []
            for j in range(4):
                s = tile * CAP + g * 4 + j
                ws.append(wbuf[slot_k[s]])
                ps.append(surf[slot_src[s]])
            lhs = jnp.concatenate(
                [
                    jnp.concatenate([ps[0], zero, ps[2], zero], axis=0),
                    jnp.concatenate([zero, ps[1], zero, ps[3]], axis=0),
                ],
                axis=1,
            ).astype(BF16)
            rhs = jnp.concatenate(
                [
                    jnp.concatenate([ws[0], ws[1]], axis=1),
                    jnp.concatenate([ws[2], ws[3]], axis=1),
                ],
                axis=0,
            )
            both = lax.dot_general(
                lhs, rhs, (((1,), (1,)), ((), ())), preferred_element_type=F32
            )
            parts = [both[0:8, :128], both[8:16, :128], both[16:24, 128:], both[24:32, 128:]]
            for j in range(4):
                send[i, pl.ds(g * 4 + j, 8, stride=CAP), :] = parts[j]
        data.start()
        return carry

    lax.fori_loop(0, TILES, produce, 0)

    mix_a, mix_b = mixes(comp)
    settle(0)
    for f in range(NF):
        sp[f, 7:8, :] = xr[0, 0, f : f + 1, :]
        sp[f, 8 + CX : 9 + CX, :] = xr[0, 1, f : f + 1, :]

    def around(box, f, i):
        return [box[f, pl.ds(pl.multiple_of(i * 8 + o, 8), 8), :] for o in (8, 0, 16)]

    def first_step(i, carry):
        rows = pl.ds(pl.multiple_of(i * 8, 8), 8)
        weight = [kc[n, rows, :] for n in range(5)]
        keep = kc[5, rows, :]
        left, right = yr[0, 0, rows, :], yr[0, 1, rows, :]
        strips = []
        for f in range(NF):
            cur, prev, nxt = around(sp, f, i)
            rate = stencil(cur, prev, nxt, left[:, f : f + 1], right[:, f : f + 1], weight)
            if f < CH:
                part[f, rows, :] = cur + (rate - (gamma[0, f] * keep) * cur)
            else:
                moved = cur + rate
                sq[f - CH, pl.ds(pl.multiple_of(i * 8 + 8, 8), 8), :] = moved
                strips.append(moved)
        pack_columns(1, i, strips)
        return carry

    lax.fori_loop(0, 16, first_step, 0)
    for f in range(CH):
        xs[1, 0, f : f + 1, :] = sq[f, 7 + CX : 8 + CX, :]
        xs[1, 1, f : f + 1, :] = sq[f, 8:9, :]
    for move in edges(1):
        move.start()
    settle(1)
    for f in range(CH):
        sq[f, 7:8, :] = xr[1, 0, f : f + 1, :]
        sq[f, 8 + CX : 9 + CX, :] = xr[1, 1, f : f + 1, :]

    def second_step(i, carry):
        rows = pl.ds(pl.multiple_of(i * 8, 8), 8)
        weight = [kc[n, rows, :] for n in range(5)]
        left, right = yr[1, 0, rows, :], yr[1, 1, rows, :]
        for f in range(CH):
            cur, prev, nxt = around(sq, f, i)
            rate = stencil(cur, prev, nxt, left[:, f : f + 1], right[:, f : f + 1], weight)
            start = sp[f + CH, pl.ds(pl.multiple_of(i * 8 + 8, 8), 8), :]
            rest[f, rows, :] = mix_a * start + (1.0 - mix_a) * cur + mix_b * rate
        return carry

    lax.fori_loop(0, 16, second_step, 0)

    def arrive(i, carry):
        data, names, _ = copies(i)
        names.wait_recv()
        data.wait_recv()
        return carry

    seg = lax.broadcasted_iota(jnp.int32, (8, 128), 1) // CAP == lax.broadcasted_iota(
        jnp.int32, (8, 128), 0
    )
    for q in range(4):
        lax.fori_loop(16 * q, 16 * q + 16, arrive, 0)
        names = []
        for half in range(2):
            first = q * 16 + half * 8
            rows = jnp.concatenate([recv_ids[first + j] for j in range(8)], axis=0)
            names.append(jnp.sum(jnp.where(seg, rows, 0.0), axis=0, keepdims=True))
        wanted = jnp.concatenate(names, axis=1)
        blocks = lax.broadcasted_iota(jnp.int32, (NB, 256), 0).astype(F32)
        select = jnp.where(blocks == wanted, 1.0, 0.0).astype(BF16)
        for c in range(0, CH, 2):
            cols = []
            for cc in (c, c + 1):
                cols.append(
                    jnp.concatenate(
                        [recv[q * 16 + j, cc * CAP : cc * CAP + CAP, :] for j in range(16)], axis=0
                    )
                )
            terms = jnp.concatenate(cols, axis=1)
            high = terms.astype(BF16)
            low = (terms - high.astype(F32)).astype(BF16)
            total = jnp.dot(select, high, preferred_element_type=F32)
            total = total + jnp.dot(select, low, preferred_element_type=F32)
            for cc in range(2):
                piece = total[:, cc * 128 : cc * 128 + 128]
                if q == 0:
                    acc[c + cc] = piece
                else:
                    acc[c + cc] += piece

    def couple(i, carry):
        rows = pl.ds(pl.multiple_of(i * 8, 8), 8)
        keep = kc[5, rows, :]
        strips = []
        for f in range(CH):
            cells = jnp.concatenate(
                [acc[f, pl.ds(pl.multiple_of(i * 32 + yb * 8, 8), 8), :] for yb in range(4)],
                axis=1,
            )
            out[f, rows, :] = cells
            moved = part[f, rows, :] + (gamma[0, f] * keep) * cells
            section[f, rows, :] = moved
            strips.append(moved)
        pack_columns(2, i, strips)
        return carry

    lax.fori_loop(0, 16, couple, 0)
    for f in range(CH):
        xs[2, 0, f : f + 1, :] = section[f, CX - 1 : CX, :]
        xs[2, 1, f : f + 1, :] = section[f, 0:1, :]
    for move in edges(2):
        move.start()

    def sent(i, carry):
        data, names, _ = copies(i)
        names.wait_send()
        data.wait_send()
        return carry

    lax.fori_loop(0, TILES, sent, 0)
    settle(2)
    for n in range(2):
        halo_x[n] = xr[2, n, 0:CH, :]
        halo_y[n] = yr[2, n]
    for e in range(3):
        for move in edges(e):
            move.wait_send()


def remap(slot_k, slot_src, gamma, ids, coefs, land, state, weights):
    smem = pl.BlockSpec(memory_space=pltpu.SMEM)
    vmem = pl.BlockSpec(memory_space=pltpu.VMEM)
    hbm = pl.BlockSpec(memory_space=pl.ANY)
    half = jax.ShapeDtypeStruct((CH, CX, CY), F32)
    return pl.pallas_call(
        remap_kernel,
        out_shape=[
            half,
            half,
            half,
            jax.ShapeDtypeStruct((2, CH, CY), F32),
            jax.ShapeDtypeStruct((2, CX, 128), F32),
        ],
        in_specs=[smem, smem, smem, vmem, vmem, vmem, hbm, hbm],
        out_specs=[vmem] * 5,
        scratch_shapes=[
            pltpu.VMEM((PAIRS, 128, 128), BF16),
            pltpu.VMEM((NB, CH, 128), F32),
            pltpu.VMEM((TILES, CH * CAP, 128), F32),
            pltpu.VMEM((TILES, CH * CAP, 128), F32),
            pltpu.VMEM((TILES, 1, 128), F32),
            pltpu.VMEM((CH, NB, 128), F32),
            pltpu.VMEM((NF, CX + 16, CY), F32),
            pltpu.VMEM((CH, CX + 16, CY), F32),
            pltpu.VMEM((CH, CX, CY), F32),
            pltpu.VMEM((6, CX, CY), F32),
            pltpu.VMEM((3, 2, NF, CY), F32),
            pltpu.VMEM((3, 2, NF, CY), F32),
            pltpu.VMEM((3, 2, CX, 128), F32),
            pltpu.VMEM((3, 2, CX, 128), F32),
            pltpu.SemaphoreType.DMA((2,)),
            pltpu.SemaphoreType.DMA((TILES,)),
            pltpu.SemaphoreType.DMA((TILES,)),
            pltpu.SemaphoreType.DMA((TILES,)),
            pltpu.SemaphoreType.DMA((TILES,)),
            pltpu.SemaphoreType.DMA((3, 4)),
            pltpu.SemaphoreType.DMA((3, 4)),
        ],
        compiler_params=pltpu.CompilerParams(
            collective_id=0, has_side_effects=True, vmem_limit_bytes=54 << 20
        ),
    )(slot_k, slot_src, gamma, ids, coefs, land, state, weights)


def finish_kernel(
    gamma, state, coefs, land, recv, section, rest, halo_x, halo_y, new, recv_out, kc
):
    f = pl.program_id(0)
    comp = lax.axis_index("comp")

    @pl.when(f == 0)
    def _():
        def prepare(i, carry):
            slopes(i, coefs, land, comp, kc)
            return carry

        lax.fori_loop(0, 16, prepare, 0)

    mix_a, mix_b = mixes(comp)
    rate_of = gamma[0, f]
    above = halo_x[0, pl.ds(f, 1), :]
    below = halo_x[1, pl.ds(f, 1), :]
    mine = lax.broadcasted_iota(jnp.int32, (8, 128), 1) == f
    for i in range(16):
        rows = pl.ds(i * 8, 8)
        weight = [kc[n, rows, :] for n in range(5)]
        keep = kc[5, rows, :]
        left = jnp.sum(jnp.where(mine, halo_y[0, rows, :], 0.0), axis=1, keepdims=True)
        right = jnp.sum(jnp.where(mine, halo_y[1, rows, :], 0.0), axis=1, keepdims=True)
        cur = section[0, rows, :]
        prev = jnp.broadcast_to(above, (8, CY)) if i == 0 else section[0, i * 8 - 8 : i * 8, :]
        nxt = (
            jnp.broadcast_to(below, (8, CY))
            if i == 15
            else section[0, i * 8 + 8 : i * 8 + 16, :]
        )
        rate = stencil(cur, prev, nxt, left, right, weight)
        cells = recv[0, rows, :]
        rate = rate + (rate_of * keep) * (cells - cur)
        new[0, 0, rows, :] = mix_a * state[0, 0, rows, :] + (1.0 - mix_a) * cur + mix_b * rate
        new[1, 0, rows, :] = rest[0, rows, :]
        recv_out[0, rows, :] = cells


def finish(gamma, state, coefs, land, recv, section, rest, halo_x, halo_y):
    field = pl.BlockSpec((1, CX, CY), lambda f: (f, 0, 0))
    return pl.pallas_call(
        finish_kernel,
        grid=(CH,),
        out_shape=[
            jax.ShapeDtypeStruct((2, CH, CX, CY), F32),
            jax.ShapeDtypeStruct((CH, CX, CY), F32),
        ],
        in_specs=[
            pl.BlockSpec(memory_space=pltpu.SMEM),
            pl.BlockSpec((1, 1, CX, CY), lambda f: (0, f, 0, 0)),
            pl.BlockSpec((1, 3, CX, CY), lambda f: (0, 0, 0, 0)),
            pl.BlockSpec((CX, CY), lambda f: (0, 0)),
            field,
            field,
            field,
            pl.BlockSpec((2, CH, CY), lambda f: (0, 0, 0)),
            pl.BlockSpec((2, CX, 128), lambda f: (0, 0, 0)),
        ],
        out_specs=[pl.BlockSpec((2, 1, CX, CY), lambda f: (0, f, 0, 0)), field],
        scratch_shapes=[pltpu.VMEM((6, CX, CY), F32)],
        compiler_params=pltpu.CompilerParams(vmem_limit_bytes=60 << 20),
    )(gamma, state, coefs, land, recv, section, rest, halo_x, halo_y)


def body(state, coefs, land_sea, gamma, pair_src, pair_dev, pair_blk, weights):
    slot_k, slot_src, slot_id = plan(
        pair_src.reshape(PAIRS), pair_dev.reshape(PAIRS), pair_blk.reshape(PAIRS)
    )
    ids = jnp.tile(slot_id.astype(F32).reshape(TILES, 1, CAP), (1, 1, 8))
    recv, section, rest, halo_x, halo_y = remap(
        slot_k, slot_src, gamma, ids, coefs, land_sea, state, weights
    )
    new, recv_out = finish(
        gamma, state, coefs, land_sea, recv, section, rest, halo_x, halo_y
    )
    return (new.reshape(1, NF, CX, CY), recv_out[None])


def solution(mesh):
    placed = (
        P("comp", None, "tx", "ty"),
        P("comp", None, "tx", "ty"),
        P("tx", "ty"),
        P("comp", None),
        P("comp", ("tx", "ty")),
        P("comp", ("tx", "ty"), None),
        P("comp", ("tx", "ty")),
        P("comp", ("tx", "ty"), None, None),
    )
    return jax.shard_map(
        body,
        mesh=mesh,
        in_specs=placed,
        out_specs=(P("comp", None, "tx", "ty"), P("comp", None, "tx", "ty")),
        check_vma=False,
    )
```

```python
import jax
import jax.numpy as jnp
from jax import lax
from jax.experimental import pallas as pl
from jax.experimental.pallas import tpu as pltpu
from jax.sharding import PartitionSpec as P

MESH = pl.DeviceIdType.MESH
F32 = jnp.float32
BF16 = jnp.bfloat16


TILES = 64
PAIRS = 512
CAP = 16
SLOTS = TILES * CAP
NB = 512
CH = 8
NF = 16
CX = 128
CY = 512


def slopes(i, coefs, land, comp, kc):
    rows = pl.ds(pl.multiple_of(i * 8, 8), 8)
    u = coefs[0, 0, rows, :]
    v = coefs[0, 1, rows, :]
    kappa = coefs[0, 2, rows, :]
    keep = jnp.where(comp == 0, 1.0, land[rows, :].astype(F32))
    kc[0, rows, :] = keep * (jnp.maximum(u, 0.0) + kappa)
    kc[1, rows, :] = keep * (kappa - jnp.minimum(u, 0.0))
    kc[2, rows, :] = keep * (jnp.maximum(v, 0.0) + kappa)
    kc[3, rows, :] = keep * (kappa - jnp.minimum(v, 0.0))
    kc[4, rows, :] = -keep * (jnp.abs(u) + jnp.abs(v) + 4.0 * kappa)
    kc[5, rows, :] = keep


def stencil(cur, prev, nxt, left, right, weight):
    sub = lax.broadcasted_iota(jnp.int32, (8, CY), 0)
    lane = lax.broadcasted_iota(jnp.int32, (8, CY), 1)
    up = jnp.where(sub == 0, pltpu.roll(prev, 1, 0), pltpu.roll(cur, 1, 0))
    down = jnp.where(sub == 7, pltpu.roll(nxt, 7, 0), pltpu.roll(cur, 7, 0))
    back = jnp.where(lane == 0, left, pltpu.roll(cur, 1, 1))
    ahead = jnp.where(lane == CY - 1, right, pltpu.roll(cur, CY - 1, 1))
    total = weight[0] * up + weight[1] * down
    total = total + (weight[2] * back + weight[3] * ahead)
    return total + weight[4] * cur


def mixes(comp):
    a = jnp.where(comp == 0, 0.0, 0.5).astype(F32)
    b = jnp.where(comp == 0, 1.0, 0.5).astype(F32)
    return a, b


def remap_kernel(
    gamma,
    src,
    dev,
    blk,
    coefs_hbm,
    land_hbm,
    state,
    weights,
    new,
    out,
    names_of,
    plan,
    table,
    rest,
    cells_of,
    coefs,
    land,
    wbuf,
    surf,
    send,
    recv,
    recv_ids,
    acc,
    sp,
    sq,
    part,
    kc,
    xs,
    xr,
    ys,
    yr,
    lsem,
    ssem,
    rsem,
    isend,
    irecv,
    esend,
    erecv,
):
    comp = lax.axis_index("comp")
    tx = lax.axis_index("tx")
    ty = lax.axis_index("ty")
    h = tx // 4
    x = tx % 4
    y = ty // 2
    core = ty % 2
    sign = 1 - 2 * core

    loads = [
        pltpu.make_async_copy(
            state.at[0, 0:CH], sp.at[0:CH, 8 : 8 + CX, :], lsem.at[0]
        ),
        pltpu.make_async_copy(weights.at[0], wbuf, lsem.at[1]),
        pltpu.make_async_copy(
            state.at[0, CH:NF], sp.at[CH:NF, 8 : 8 + CX, :], lsem.at[2]
        ),
    ]
    loads.append(pltpu.make_async_copy(coefs_hbm, coefs, lsem.at[4]))
    loads.append(pltpu.make_async_copy(land_hbm, land, lsem.at[5]))
    for n in (0, 3, 4, 1, 2):
        loads[n].start()

    def partner(i):
        dh = lax.rem(i, 2)
        dx = lax.rem(lax.div(i, 2), 4)
        dy = lax.rem(lax.div(i, 8) + dx, 4)
        dc = lax.div(i, 32)
        to_x = lax.rem(h + dh, 2) * 4 + lax.rem(x + sign * dx + 4, 4)
        to_y = lax.rem(y + sign * dy + 4, 4) * 2 + lax.rem(core + dc, 2)
        return to_x, to_y

    beside = (
        (comp, lax.rem(tx + 1, 8), ty),
        (comp, lax.rem(tx + 7, 8), ty),
        (comp, tx, lax.rem(ty + 1, 8)),
        (comp, tx, lax.rem(ty + 7, 8)),
    )

    barrier = pltpu.get_barrier_semaphore()

    for to in beside:
        pl.semaphore_signal(barrier, 1, device_id=to, device_id_type=MESH)

    def prepare(i, carry):
        for j in range(4):
            to_x, to_y = partner(i * 4 + j)
            pl.semaphore_signal(barrier, 1, device_id=(1 - comp, to_x, to_y), device_id_type=MESH)
        slopes(i, coefs, land, comp, kc)
        return carry

    loads[3].wait()
    loads[4].wait()
    lax.fori_loop(0, 16, prepare, 0)

    target = dev[...]
    member = lax.broadcasted_iota(jnp.int32, (TILES, PAIRS), 0) == target
    one_of = jnp.where(member, 1.0, 0.0).astype(BF16)
    before = jnp.where(
        lax.broadcasted_iota(jnp.int32, (PAIRS, PAIRS), 0)
        < lax.broadcasted_iota(jnp.int32, (PAIRS, PAIRS), 1),
        1.0,
        0.0,
    ).astype(BF16)
    counted = jnp.dot(one_of, before, preferred_element_type=F32)
    rank = jnp.sum(jnp.where(member, counted, 0.0), axis=0, keepdims=True)
    at_rank = lax.broadcasted_iota(jnp.int32, (128, PAIRS), 0) % CAP
    at_rank = jnp.where(at_rank.astype(F32) == rank, 1.0, 0.0).astype(BF16)
    number = lax.broadcasted_iota(jnp.int32, (1, PAIRS), 1)
    b = blk[...]
    b = (b // 32) * 32 + (b % 4) * 8 + (b // 4) % 8

    def tabled(value):
        rows = jnp.where(member, value.astype(F32), 0.0).astype(BF16)
        return lax.dot_general(
            rows, at_rank, (((1,), (1,)), ((), ())), preferred_element_type=F32
        )

    def placed(value):
        return 2.0 * tabled(value // 2) + tabled(value % 2)

    table[0] = placed(number).astype(jnp.int32)
    table[1] = placed(src[...]).astype(jnp.int32)
    to_smem = pltpu.make_async_copy(table, plan, lsem.at[3])
    to_smem.start()
    names = placed(b) + float(NB) * (1.0 - tabled(jnp.ones((1, PAIRS), jnp.int32)))
    for d in range(TILES):
        names_of[d] = names[d : d + 1, :]
    loads[0].wait()

    def relay(i, carry):
        for yb in range(4):
            rows = pl.ds(pl.multiple_of(i * 8 + 8, 8), 8)
            tiles = sp[0:CH, rows, yb * 128 : yb * 128 + 128]
            tiles = jnp.swapaxes(tiles, 0, 1)
            for r in range(8):
                surf[i * 32 + r * 4 + yb] = tiles[r]
        return carry

    lax.fori_loop(0, 16, relay, 0)

    def edges(e):
        moves = []
        for n in range(4):
            count = NF if e == 0 else CH
            if n < 2:
                box = (xs.at[e, n, 0:count], xr.at[e, n, 0:count])
            else:
                box = (ys.at[e, n - 2], yr.at[e, n - 2])
            moves.append(
                pltpu.make_async_remote_copy(
                    box[0],
                    box[1],
                    esend.at[e, n],
                    erecv.at[e, n],
                    device_id=beside[n],
                    device_id_type=MESH,
                )
            )
        return moves

    lanes = lax.broadcasted_iota(jnp.int32, (8, 128), 1)

    def pack_columns(e, i, strips):
        first = jnp.zeros((8, 128), F32)
        last = jnp.zeros((8, 128), F32)
        for f, cells in enumerate(strips):
            first = jnp.where(lanes == f, cells[:, 0:1], first)
            last = jnp.where(lanes == f, cells[:, -1:], last)
        rows = pl.ds(pl.multiple_of(i * 8, 8), 8)
        ys[e, 0, rows, :] = last
        ys[e, 1, rows, :] = first

    def settle(e):
        for move in edges(e):
            move.wait_recv()
        for n, (place, end) in enumerate(((tx, 0), (tx, 7))):
            count = NF if e == 0 else CH
            xr[e, n, 0:count] = jnp.where(place == end, 0.0, xr[e, n, 0:count])
        for n, (place, end) in enumerate(((ty, 0), (ty, 7))):
            yr[e, n] = jnp.where(place == end, 0.0, yr[e, n])

    def copies(i):
        to_x, to_y = partner(i)
        to = (1 - comp, to_x, to_y)
        data = pltpu.make_async_remote_copy(
            send.at[i], recv.at[i], ssem.at[i], rsem.at[i], device_id=to, device_id_type=MESH
        )
        names = pltpu.make_async_remote_copy(
            names_of.at[to_x * 8 + to_y],
            recv_ids.at[i],
            isend.at[i],
            irecv.at[i],
            device_id=to,
            device_id_type=MESH,
        )
        return data, names, to_x * 8 + to_y

    to_smem.wait()
    loads[1].wait()
    pl.semaphore_wait(barrier, TILES + 4)

    def produce(i, carry):
        data, names, tile = copies(i)
        names.start()
        zero = jnp.zeros((8, 128), F32)
        for g in range(CAP // 4):
            ws = []
            ps = []
            for j in range(4):
                ws.append(wbuf[jnp.clip(plan[0, tile, g * 4 + j], 0, PAIRS - 1)])
                ps.append(surf[jnp.clip(plan[1, tile, g * 4 + j], 0, NB - 1)])
            lhs = jnp.concatenate(
                [
                    jnp.concatenate([ps[0], zero, ps[2], zero], axis=0),
                    jnp.concatenate([zero, ps[1], zero, ps[3]], axis=0),
                ],
                axis=1,
            ).astype(BF16)
            rhs = jnp.concatenate(
                [
                    jnp.concatenate([ws[0], ws[1]], axis=1),
                    jnp.concatenate([ws[2], ws[3]], axis=1),
                ],
                axis=0,
            )
            both = lax.dot_general(
                lhs, rhs, (((1,), (1,)), ((), ())), preferred_element_type=F32
            )
            parts = [both[0:8, :128], both[8:16, :128], both[16:24, 128:], both[24:32, 128:]]
            for j in range(4):
                send[i, pl.ds(g * 4 + j, 8, stride=CAP), :] = parts[j]
        data.start()
        return carry

    lax.fori_loop(0, 8, produce, 0)
    loads[2].wait()

    def pack_state(i, carry):
        rows = pl.ds(pl.multiple_of(i * 8 + 8, 8), 8)
        pack_columns(0, i, [sp[f, rows, :] for f in range(NF)])
        return carry

    lax.fori_loop(0, 16, pack_state, 0)
    for f in range(NF):
        xs[0, 0, f : f + 1, :] = sp[f, 7 + CX : 8 + CX, :]
        xs[0, 1, f : f + 1, :] = sp[f, 8:9, :]

    for move in edges(0):
        move.start()

    lax.fori_loop(8, 40, produce, 0)

    mix_a, mix_b = mixes(comp)
    settle(0)
    for f in range(NF):
        sp[f, 7:8, :] = xr[0, 0, f : f + 1, :]
        sp[f, 8 + CX : 9 + CX, :] = xr[0, 1, f : f + 1, :]

    def around(box, f, i):
        return [box[f, pl.ds(pl.multiple_of(i * 8 + o, 8), 8), :] for o in (8, 0, 16)]

    def first_step(i, carry):
        rows = pl.ds(pl.multiple_of(i * 8, 8), 8)
        weight = [kc[n, rows, :] for n in range(5)]
        keep = kc[5, rows, :]
        left, right = yr[0, 0, rows, :], yr[0, 1, rows, :]
        strips = []
        for f in range(NF):
            cur, prev, nxt = around(sp, f, i)
            rate = stencil(cur, prev, nxt, left[:, f : f + 1], right[:, f : f + 1], weight)
            if f < CH:
                part[f, rows, :] = cur + (rate - (gamma[0, f] * keep) * cur)
            else:
                moved = cur + rate
                sq[f - CH, pl.ds(pl.multiple_of(i * 8 + 8, 8), 8), :] = moved
                strips.append(moved)
        pack_columns(1, i, strips)
        return carry

    lax.fori_loop(0, 16, first_step, 0)
    for f in range(CH):
        xs[1, 0, f : f + 1, :] = sq[f, 7 + CX : 8 + CX, :]
        xs[1, 1, f : f + 1, :] = sq[f, 8:9, :]
    for move in edges(1):
        move.start()
    lax.fori_loop(40, TILES, produce, 0)
    settle(1)
    for f in range(CH):
        sq[f, 7:8, :] = xr[1, 0, f : f + 1, :]
        sq[f, 8 + CX : 9 + CX, :] = xr[1, 1, f : f + 1, :]

    def second_step(i, carry):
        rows = pl.ds(pl.multiple_of(i * 8, 8), 8)
        weight = [kc[n, rows, :] for n in range(5)]
        left, right = yr[1, 0, rows, :], yr[1, 1, rows, :]
        for f in range(CH):
            cur, prev, nxt = around(sq, f, i)
            rate = stencil(cur, prev, nxt, left[:, f : f + 1], right[:, f : f + 1], weight)
            start = sp[f + CH, pl.ds(pl.multiple_of(i * 8 + 8, 8), 8), :]
            rest[f, rows, :] = mix_a * start + (1.0 - mix_a) * cur + mix_b * rate
        return carry

    lax.fori_loop(0, 16, second_step, 0)
    stores = [pltpu.make_async_copy(rest, new.at[0, CH:NF], lsem.at[0])]
    stores[0].start()

    def arrive(i, carry):
        data, names, _ = copies(i)
        names.wait_recv()
        data.wait_recv()
        return carry

    seg = lax.broadcasted_iota(jnp.int32, (8, 128), 1) // CAP == lax.broadcasted_iota(
        jnp.int32, (8, 128), 0
    )
    for q in range(4):
        lax.fori_loop(16 * q, 16 * q + 16, arrive, 0)
        names = []
        for half in range(2):
            first = q * 16 + half * 8
            rows = jnp.concatenate([recv_ids[first + j] for j in range(8)], axis=0)
            names.append(jnp.sum(jnp.where(seg, rows, 0.0), axis=0, keepdims=True))
        wanted = jnp.concatenate(names, axis=1)
        blocks = lax.broadcasted_iota(jnp.int32, (NB, 256), 0).astype(F32)
        select = jnp.where(blocks == wanted, 1.0, 0.0).astype(BF16)
        for c in range(0, CH, 2):
            cols = []
            for cc in (c, c + 1):
                cols.append(
                    jnp.concatenate(
                        [recv[q * 16 + j, cc * CAP : cc * CAP + CAP, :] for j in range(16)], axis=0
                    )
                )
            terms = jnp.concatenate(cols, axis=1)
            high = terms.astype(BF16)
            low = (terms - high.astype(F32)).astype(BF16)
            total = jnp.dot(select, high, preferred_element_type=F32)
            total = total + jnp.dot(select, low, preferred_element_type=F32)
            for cc in range(2):
                piece = total[:, cc * 128 : cc * 128 + 128]
                if q == 0:
                    acc[c + cc] = piece
                else:
                    acc[c + cc] += piece

    def couple(i, carry):
        rows = pl.ds(pl.multiple_of(i * 8, 8), 8)
        keep = kc[5, rows, :]
        strips = []
        for f in range(CH):
            cells = jnp.concatenate(
                [acc[f, pl.ds(pl.multiple_of(i * 32 + yb * 8, 8), 8), :] for yb in range(4)],
                axis=1,
            )
            cells_of[f, rows, :] = cells
            moved = part[f, rows, :] + (gamma[0, f] * keep) * cells
            sq[f, pl.ds(pl.multiple_of(i * 8 + 8, 8), 8), :] = moved
            strips.append(moved)
        pack_columns(2, i, strips)
        return carry

    lax.fori_loop(0, 16, couple, 0)
    for f in range(CH):
        xs[2, 0, f : f + 1, :] = sq[f, 7 + CX : 8 + CX, :]
        xs[2, 1, f : f + 1, :] = sq[f, 8:9, :]
    for move in edges(2):
        move.start()
    stores.append(pltpu.make_async_copy(cells_of, out.at[0], lsem.at[1]))
    stores[1].start()

    def sent(i, carry):
        data, names, _ = copies(i)
        names.wait_send()
        data.wait_send()
        return carry

    lax.fori_loop(0, TILES, sent, 0)
    settle(2)
    for f in range(CH):
        sq[f, 7:8, :] = xr[2, 0, f : f + 1, :]
        sq[f, 8 + CX : 9 + CX, :] = xr[2, 1, f : f + 1, :]

    def last_step(i, carry):
        rows = pl.ds(pl.multiple_of(i * 8, 8), 8)
        weight = [kc[n, rows, :] for n in range(5)]
        keep = kc[5, rows, :]
        left, right = yr[2, 0, rows, :], yr[2, 1, rows, :]
        for f in range(CH):
            cur, prev, nxt = around(sq, f, i)
            rate = stencil(cur, prev, nxt, left[:, f : f + 1], right[:, f : f + 1], weight)
            rate = rate + (gamma[0, f] * keep) * (cells_of[f, rows, :] - cur)
            start = sp[f, pl.ds(pl.multiple_of(i * 8 + 8, 8), 8), :]
            part[f, rows, :] = mix_a * start + (1.0 - mix_a) * cur + mix_b * rate
        return carry

    for q in range(4):
        lax.fori_loop(4 * q, 4 * q + 4, last_step, 0)
        rows = pl.ds(32 * q, 32)
        store = pltpu.make_async_copy(
            part.at[:, rows, :], new.at[0, 0:CH, rows, :], lsem.at[2 + q]
        )
        store.start()
        stores.append(store)
    for e in range(3):
        for move in edges(e):
            move.wait_send()
    for store in stores:
        store.wait()


def remap(gamma, src, dev, blk, coefs, land, state, weights):
    smem = pl.BlockSpec(memory_space=pltpu.SMEM)
    vmem = pl.BlockSpec(memory_space=pltpu.VMEM)
    hbm = pl.BlockSpec(memory_space=pl.ANY)
    return pl.pallas_call(
        remap_kernel,
        out_shape=[
            jax.ShapeDtypeStruct((1, NF, CX, CY), F32),
            jax.ShapeDtypeStruct((1, CH, CX, CY), F32),
        ],
        in_specs=[smem, vmem, vmem, vmem, hbm, hbm, hbm, hbm],
        out_specs=[hbm] * 2,
        scratch_shapes=[
            pltpu.VMEM((TILES, 1, 128), F32),
            pltpu.SMEM((2, TILES, 128), jnp.int32),
            pltpu.VMEM((2, TILES, 128), jnp.int32),
            pltpu.VMEM((CH, CX, CY), F32),
            pltpu.VMEM((CH, CX, CY), F32),
            pltpu.VMEM((1, 3, CX, CY), F32),
            pltpu.VMEM((CX, CY), jnp.int32),
            pltpu.VMEM((PAIRS, 128, 128), BF16),
            pltpu.VMEM((NB, CH, 128), F32),
            pltpu.VMEM((TILES, CH * CAP, 128), F32),
            pltpu.VMEM((TILES, CH * CAP, 128), F32),
            pltpu.VMEM((TILES, 1, 128), F32),
            pltpu.VMEM((CH, NB, 128), F32),
            pltpu.VMEM((NF, CX + 16, CY), F32),
            pltpu.VMEM((CH, CX + 16, CY), F32),
            pltpu.VMEM((CH, CX, CY), F32),
            pltpu.VMEM((6, CX, CY), F32),
            pltpu.VMEM((3, 2, NF, CY), F32),
            pltpu.VMEM((3, 2, NF, CY), F32),
            pltpu.VMEM((3, 2, CX, 128), F32),
            pltpu.VMEM((3, 2, CX, 128), F32),
            pltpu.SemaphoreType.DMA((6,)),
            pltpu.SemaphoreType.DMA((TILES,)),
            pltpu.SemaphoreType.DMA((TILES,)),
            pltpu.SemaphoreType.DMA((TILES,)),
            pltpu.SemaphoreType.DMA((TILES,)),
            pltpu.SemaphoreType.DMA((3, 4)),
            pltpu.SemaphoreType.DMA((3, 4)),
        ],
        compiler_params=pltpu.CompilerParams(
            collective_id=0, has_side_effects=True, vmem_limit_bytes=56 << 20
        ),
    )(gamma, src, dev, blk, coefs, land, state, weights)


def body(state, coefs, land_sea, gamma, pair_src, pair_dev, pair_blk, weights):
    return remap(
        gamma,
        pair_src,
        pair_dev.reshape(1, PAIRS),
        pair_blk,
        coefs,
        land_sea,
        state,
        weights,
    )


def solution(mesh):
    placed = (
        P("comp", None, "tx", "ty"),
        P("comp", None, "tx", "ty"),
        P("tx", "ty"),
        P("comp", None),
        P("comp", ("tx", "ty")),
        P("comp", ("tx", "ty"), None),
        P("comp", ("tx", "ty")),
        P("comp", ("tx", "ty"), None, None),
    )
    return jax.shard_map(
        body,
        mesh=mesh,
        in_specs=placed,
        out_specs=(P("comp", None, "tx", "ty"), P("comp", None, "tx", "ty")),
        check_vma=False,
    )
```

```python
import jax
import jax.numpy as jnp
from jax import lax
from jax.experimental import pallas as pl
from jax.experimental.pallas import tpu as pltpu
from jax.sharding import PartitionSpec as P

MESH = pl.DeviceIdType.MESH
F32 = jnp.float32
BF16 = jnp.bfloat16


TILES = 64
PAIRS = 512
CAP = 16
SLOTS = TILES * CAP
NB = 512
CH = 8
NF = 16
CX = 128
CY = 512


def slopes(rows, coefs, land, comp):
    u = coefs[0, 0, rows, :]
    v = coefs[0, 1, rows, :]
    kappa = coefs[0, 2, rows, :]
    keep = jnp.where(comp == 0, 1.0, land[rows, :].astype(F32))
    return [
        keep * (jnp.maximum(u, 0.0) + kappa),
        keep * (kappa - jnp.minimum(u, 0.0)),
        keep * (jnp.maximum(v, 0.0) + kappa),
        keep * (kappa - jnp.minimum(v, 0.0)),
        -keep * (jnp.abs(u) + jnp.abs(v) + 4.0 * kappa),
        keep,
    ]


def stencil(cur, prev, nxt, left, right, weight):
    sub = lax.broadcasted_iota(jnp.int32, (8, CY), 0)
    lane = lax.broadcasted_iota(jnp.int32, (8, CY), 1)
    up = jnp.where(sub == 0, pltpu.roll(prev, 1, 0), pltpu.roll(cur, 1, 0))
    down = jnp.where(sub == 7, pltpu.roll(nxt, 7, 0), pltpu.roll(cur, 7, 0))
    back = jnp.where(lane == 0, left, pltpu.roll(cur, 1, 1))
    ahead = jnp.where(lane == CY - 1, right, pltpu.roll(cur, CY - 1, 1))
    total = weight[0] * up + weight[1] * down
    total = total + (weight[2] * back + weight[3] * ahead)
    return total + weight[4] * cur


def mixes(comp):
    a = jnp.where(comp == 0, 0.0, 0.5).astype(F32)
    b = jnp.where(comp == 0, 1.0, 0.5).astype(F32)
    return a, b


def remap_kernel(
    gamma,
    src,
    dev,
    blk,
    coefs_hbm,
    land_hbm,
    state,
    weights,
    out,
    section,
    others,
    halo_x,
    halo_y,
    names_of,
    plan,
    table,
    rest,
    cells_of,
    coefs,
    land,
    wbuf,
    surf,
    send,
    recv,
    recv_ids,
    acc,
    sp,
    sq,
    part,
    kc,
    xs,
    xr,
    ys,
    yr,
    lsem,
    ssem,
    rsem,
    isend,
    irecv,
    esend,
    erecv,
):
    comp = lax.axis_index("comp")
    tx = lax.axis_index("tx")
    ty = lax.axis_index("ty")
    h = tx // 4
    x = tx % 4
    y = ty // 2
    core = ty % 2
    sign = 1 - 2 * core

    loads = [
        pltpu.make_async_copy(
            state.at[0, 0:CH], sp.at[0:CH, 8 : 8 + CX, :], lsem.at[0]
        ),
        pltpu.make_async_copy(weights.at[0], wbuf, lsem.at[1]),
        pltpu.make_async_copy(
            state.at[0, CH:NF], sp.at[CH:NF, 8 : 8 + CX, :], lsem.at[2]
        ),
    ]
    loads.append(pltpu.make_async_copy(coefs_hbm, coefs, lsem.at[4]))
    loads.append(pltpu.make_async_copy(land_hbm, land, lsem.at[5]))
    for n in (0, 1, 3, 4, 2):
        loads[n].start()

    def partner(i):
        dh = lax.rem(i, 2)
        dx = lax.rem(lax.div(i, 2), 4)
        dy = lax.rem(lax.div(i, 8) + dx, 4)
        dc = lax.div(i, 32)
        to_x = lax.rem(h + dh, 2) * 4 + lax.rem(x + sign * dx + 4, 4)
        to_y = lax.rem(y + sign * dy + 4, 4) * 2 + lax.rem(core + dc, 2)
        return to_x, to_y

    beside = (
        (comp, lax.rem(tx + 1, 8), ty),
        (comp, lax.rem(tx + 7, 8), ty),
        (comp, tx, lax.rem(ty + 1, 8)),
        (comp, tx, lax.rem(ty + 7, 8)),
    )

    barrier = pltpu.get_barrier_semaphore()

    for to in beside:
        pl.semaphore_signal(barrier, 1, device_id=to, device_id_type=MESH)

    to_xs = [
        lax.rem(h + dh, 2) * 4 + lax.rem(x + sign * dx + 4, 4) for dh in range(2) for dx in range(4)
    ]
    to_ys = [
        lax.rem(y + sign * dy + 4, 4) * 2 + lax.rem(core + dc, 2) for dy in range(4) for dc in range(2)
    ]
    for to_x in to_xs:
        for to_y in to_ys:
            pl.semaphore_signal(barrier, 1, device_id=(1 - comp, to_x, to_y), device_id_type=MESH)

    target = dev[...]
    member = lax.broadcasted_iota(jnp.int32, (TILES, PAIRS), 0) == target
    one_of = jnp.where(member, 1.0, 0.0).astype(BF16)
    before = jnp.where(
        lax.broadcasted_iota(jnp.int32, (PAIRS, PAIRS), 0)
        < lax.broadcasted_iota(jnp.int32, (PAIRS, PAIRS), 1),
        1.0,
        0.0,
    ).astype(BF16)
    counted = jnp.dot(one_of, before, preferred_element_type=F32)
    rank = jnp.sum(jnp.where(member, counted, 0.0), axis=0, keepdims=True)
    at_rank = lax.broadcasted_iota(jnp.int32, (128, PAIRS), 0) % CAP
    at_rank = jnp.where(at_rank.astype(F32) == rank, 1.0, 0.0).astype(BF16)
    number = lax.broadcasted_iota(jnp.int32, (1, PAIRS), 1)
    b = blk[...]
    b = (b // 32) * 32 + (b % 4) * 8 + (b // 4) % 8

    def tabled(value):
        rows = jnp.where(member, value.astype(F32), 0.0).astype(BF16)
        return lax.dot_general(
            rows, at_rank, (((1,), (1,)), ((), ())), preferred_element_type=F32
        )

    def placed(value):
        return 2.0 * tabled(value // 2) + tabled(value % 2)

    table[0] = placed(number).astype(jnp.int32)
    table[1] = placed(src[...]).astype(jnp.int32)
    to_smem = pltpu.make_async_copy(table, plan, lsem.at[3])
    to_smem.start()
    names = placed(b) + float(NB) * (1.0 - tabled(jnp.ones((1, PAIRS), jnp.int32)))
    for d in range(TILES):
        names_of[d] = names[d : d + 1, :]
    loads[0].wait()

    def relay(i, carry):
        for yb in range(4):
            rows = pl.ds(pl.multiple_of(i * 8 + 8, 8), 8)
            tiles = sp[0:CH, rows, yb * 128 : yb * 128 + 128]
            tiles = jnp.swapaxes(tiles, 0, 1)
            for r in range(8):
                surf[i * 32 + r * 4 + yb] = tiles[r]
        return carry

    lax.fori_loop(0, 16, relay, 0)

    def edges(e):
        moves = []
        for n in range(4):
            count = NF if e == 0 else CH
            if n < 2:
                box = (xs.at[e, n, 0:count], xr.at[e, n, 0:count])
            else:
                box = (ys.at[e, n - 2], yr.at[e, n - 2])
            moves.append(
                pltpu.make_async_remote_copy(
                    box[0],
                    box[1],
                    esend.at[e, n],
                    erecv.at[e, n],
                    device_id=beside[n],
                    device_id_type=MESH,
                )
            )
        return moves

    lanes = lax.broadcasted_iota(jnp.int32, (8, 128), 1)

    def pack_columns(e, i, strips):
        first = jnp.zeros((8, 128), F32)
        last = jnp.zeros((8, 128), F32)
        for f, cells in enumerate(strips):
            first = jnp.where(lanes == f, cells[:, 0:1], first)
            last = jnp.where(lanes == f, cells[:, -1:], last)
        rows = pl.ds(pl.multiple_of(i * 8, 8), 8)
        ys[e, 0, rows, :] = last
        ys[e, 1, rows, :] = first

    def settle(e):
        for move in edges(e):
            move.wait_recv()
        for n, (place, end) in enumerate(((tx, 0), (tx, 7))):
            count = NF if e == 0 else CH
            xr[e, n, 0:count] = jnp.where(place == end, 0.0, xr[e, n, 0:count])
        for n, (place, end) in enumerate(((ty, 0), (ty, 7))):
            yr[e, n] = jnp.where(place == end, 0.0, yr[e, n])

    def copies(i):
        to_x, to_y = partner(i)
        to = (1 - comp, to_x, to_y)
        data = pltpu.make_async_remote_copy(
            send.at[i], recv.at[i], ssem.at[i], rsem.at[i], device_id=to, device_id_type=MESH
        )
        names = pltpu.make_async_remote_copy(
            names_of.at[to_x * 8 + to_y],
            recv_ids.at[i],
            isend.at[i],
            irecv.at[i],
            device_id=to,
            device_id_type=MESH,
        )
        return data, names, to_x * 8 + to_y

    to_smem.wait()
    loads[1].wait()
    pl.semaphore_wait(barrier, TILES + 4)

    def produce(i, carry):
        data, names, tile = copies(i)
        names.start()
        zero = jnp.zeros((8, 128), F32)
        for g in range(CAP // 4):
            ws = []
            ps = []
            for j in range(4):
                ws.append(wbuf[jnp.clip(plan[0, tile, g * 4 + j], 0, PAIRS - 1)])
                ps.append(surf[jnp.clip(plan[1, tile, g * 4 + j], 0, NB - 1)])
            lhs = jnp.concatenate(
                [
                    jnp.concatenate([ps[0], zero, ps[2], zero], axis=0),
                    jnp.concatenate([zero, ps[1], zero, ps[3]], axis=0),
                ],
                axis=1,
            ).astype(BF16)
            rhs = jnp.concatenate(
                [
                    jnp.concatenate([ws[0], ws[1]], axis=1),
                    jnp.concatenate([ws[2], ws[3]], axis=1),
                ],
                axis=0,
            )
            both = lax.dot_general(
                lhs, rhs, (((1,), (1,)), ((), ())), preferred_element_type=F32
            )
            parts = [both[0:8, :128], both[8:16, :128], both[16:24, 128:], both[24:32, 128:]]
            for j in range(4):
                send[i, pl.ds(g * 4 + j, 8, stride=CAP), :] = parts[j]
        data.start()
        return carry

    lax.fori_loop(0, 8, produce, 0)
    loads[2].wait()

    def prepare(i, carry):
        rows = pl.ds(pl.multiple_of(i * 8, 8), 8)
        for n, value in enumerate(slopes(rows, coefs, land, comp)):
            kc[n, rows, :] = value
        return carry

    loads[3].wait()
    loads[4].wait()
    lax.fori_loop(0, 16, prepare, 0)

    def pack_state(i, carry):
        rows = pl.ds(pl.multiple_of(i * 8 + 8, 8), 8)
        pack_columns(0, i, [sp[f, rows, :] for f in range(NF)])
        return carry

    lax.fori_loop(0, 16, pack_state, 0)
    for f in range(NF):
        xs[0, 0, f : f + 1, :] = sp[f, 7 + CX : 8 + CX, :]
        xs[0, 1, f : f + 1, :] = sp[f, 8:9, :]

    for move in edges(0):
        move.start()

    lax.fori_loop(8, 40, produce, 0)

    mix_a, mix_b = mixes(comp)
    settle(0)
    for f in range(NF):
        sp[f, 7:8, :] = xr[0, 0, f : f + 1, :]
        sp[f, 8 + CX : 9 + CX, :] = xr[0, 1, f : f + 1, :]

    def around(box, f, i):
        return [box[f, pl.ds(pl.multiple_of(i * 8 + o, 8), 8), :] for o in (8, 0, 16)]

    def first_step(i, carry):
        rows = pl.ds(pl.multiple_of(i * 8, 8), 8)
        weight = [kc[n, rows, :] for n in range(5)]
        keep = kc[5, rows, :]
        left, right = yr[0, 0, rows, :], yr[0, 1, rows, :]
        strips = []
        for f in range(NF):
            cur, prev, nxt = around(sp, f, i)
            rate = stencil(cur, prev, nxt, left[:, f : f + 1], right[:, f : f + 1], weight)
            if f < CH:
                part[f, rows, :] = cur + (rate - (gamma[0, f] * keep) * cur)
            else:
                moved = cur + rate
                sq[f - CH, pl.ds(pl.multiple_of(i * 8 + 8, 8), 8), :] = moved
                strips.append(moved)
        pack_columns(1, i, strips)
        return carry

    lax.fori_loop(0, 16, first_step, 0)
    for f in range(CH):
        xs[1, 0, f : f + 1, :] = sq[f, 7 + CX : 8 + CX, :]
        xs[1, 1, f : f + 1, :] = sq[f, 8:9, :]
    for move in edges(1):
        move.start()
    lax.fori_loop(40, TILES, produce, 0)
    settle(1)
    for f in range(CH):
        sq[f, 7:8, :] = xr[1, 0, f : f + 1, :]
        sq[f, 8 + CX : 9 + CX, :] = xr[1, 1, f : f + 1, :]

    def second_step(i, carry):
        rows = pl.ds(pl.multiple_of(i * 8, 8), 8)
        weight = [kc[n, rows, :] for n in range(5)]
        left, right = yr[1, 0, rows, :], yr[1, 1, rows, :]
        for f in range(CH):
            cur, prev, nxt = around(sq, f, i)
            rate = stencil(cur, prev, nxt, left[:, f : f + 1], right[:, f : f + 1], weight)
            start = sp[f + CH, pl.ds(pl.multiple_of(i * 8 + 8, 8), 8), :]
            rest[f, rows, :] = mix_a * start + (1.0 - mix_a) * cur + mix_b * rate
        return carry

    lax.fori_loop(0, 16, second_step, 0)
    stores = [pltpu.make_async_copy(rest, others, lsem.at[0])]
    stores[0].start()

    def arrive(i, carry):
        data, names, _ = copies(i)
        names.wait_recv()
        data.wait_recv()
        return carry

    seg = lax.broadcasted_iota(jnp.int32, (8, 128), 1) // CAP == lax.broadcasted_iota(
        jnp.int32, (8, 128), 0
    )
    for q in range(4):
        lax.fori_loop(16 * q, 16 * q + 16, arrive, 0)
        names = []
        for half in range(2):
            first = q * 16 + half * 8
            rows = jnp.concatenate([recv_ids[first + j] for j in range(8)], axis=0)
            names.append(jnp.sum(jnp.where(seg, rows, 0.0), axis=0, keepdims=True))
        wanted = jnp.concatenate(names, axis=1)
        blocks = lax.broadcasted_iota(jnp.int32, (NB, 256), 0).astype(F32)
        select = jnp.where(blocks == wanted, 1.0, 0.0).astype(BF16)
        for c in range(0, CH, 2):
            cols = []
            for cc in (c, c + 1):
                cols.append(
                    jnp.concatenate(
                        [recv[q * 16 + j, cc * CAP : cc * CAP + CAP, :] for j in range(16)], axis=0
                    )
                )
            terms = jnp.concatenate(cols, axis=1)
            high = terms.astype(BF16)
            low = (terms - high.astype(F32)).astype(BF16)
            total = jnp.dot(select, high, preferred_element_type=F32)
            total = total + jnp.dot(select, low, preferred_element_type=F32)
            for cc in range(2):
                piece = total[:, cc * 128 : cc * 128 + 128]
                if q == 0:
                    acc[c + cc] = piece
                else:
                    acc[c + cc] += piece

    def couple(i, carry):
        rows = pl.ds(pl.multiple_of(i * 8, 8), 8)
        keep = kc[5, rows, :]
        strips = []
        for f in range(CH):
            cells = jnp.concatenate(
                [acc[f, pl.ds(pl.multiple_of(i * 32 + yb * 8, 8), 8), :] for yb in range(4)],
                axis=1,
            )
            cells_of[f, rows, :] = cells
            moved = part[f, rows, :] + (gamma[0, f] * keep) * cells
            sq[f, pl.ds(pl.multiple_of(i * 8 + 8, 8), 8), :] = moved
            strips.append(moved)
        pack_columns(2, i, strips)
        return carry

    lax.fori_loop(0, 16, couple, 0)
    for f in range(CH):
        xs[2, 0, f : f + 1, :] = sq[f, 7 + CX : 8 + CX, :]
        xs[2, 1, f : f + 1, :] = sq[f, 8:9, :]
    for move in edges(2):
        move.start()
    stores.append(
        pltpu.make_async_copy(sq.at[:, 8 : 8 + CX, :], section, lsem.at[2])
    )
    stores.append(pltpu.make_async_copy(cells_of, out, lsem.at[1]))
    for store in stores[1:]:
        store.start()

    def sent(i, carry):
        data, names, _ = copies(i)
        names.wait_send()
        data.wait_send()
        return carry

    lax.fori_loop(0, TILES, sent, 0)
    settle(2)
    for copy in (
        pltpu.make_async_copy(xr.at[2, :, 0:CH, :], halo_x, lsem.at[3]),
        pltpu.make_async_copy(yr.at[2], halo_y, lsem.at[4]),
    ):
        copy.start()
        stores.append(copy)
    for e in range(3):
        for move in edges(e):
            move.wait_send()
    for store in stores:
        store.wait()


def remap(gamma, src, dev, blk, coefs, land, state, weights):
    smem = pl.BlockSpec(memory_space=pltpu.SMEM)
    vmem = pl.BlockSpec(memory_space=pltpu.VMEM)
    hbm = pl.BlockSpec(memory_space=pl.ANY)
    half = jax.ShapeDtypeStruct((CH, CX, CY), F32)
    return pl.pallas_call(
        remap_kernel,
        out_shape=[
            half,
            half,
            half,
            jax.ShapeDtypeStruct((2, CH, CY), F32),
            jax.ShapeDtypeStruct((2, CX, 128), F32),
        ],
        in_specs=[smem, vmem, vmem, vmem, hbm, hbm, hbm, hbm],
        out_specs=[hbm] * 5,
        scratch_shapes=[
            pltpu.VMEM((TILES, 1, 128), F32),
            pltpu.SMEM((2, TILES, 128), jnp.int32),
            pltpu.VMEM((2, TILES, 128), jnp.int32),
            pltpu.VMEM((CH, CX, CY), F32),
            pltpu.VMEM((CH, CX, CY), F32),
            pltpu.VMEM((1, 3, CX, CY), F32),
            pltpu.VMEM((CX, CY), jnp.int32),
            pltpu.VMEM((PAIRS, 128, 128), BF16),
            pltpu.VMEM((NB, CH, 128), F32),
            pltpu.VMEM((TILES, CH * CAP, 128), F32),
            pltpu.VMEM((TILES, CH * CAP, 128), F32),
            pltpu.VMEM((TILES, 1, 128), F32),
            pltpu.VMEM((CH, NB, 128), F32),
            pltpu.VMEM((NF, CX + 16, CY), F32),
            pltpu.VMEM((CH, CX + 16, CY), F32),
            pltpu.VMEM((CH, CX, CY), F32),
            pltpu.VMEM((6, CX, CY), F32),
            pltpu.VMEM((3, 2, NF, CY), F32),
            pltpu.VMEM((3, 2, NF, CY), F32),
            pltpu.VMEM((3, 2, CX, 128), F32),
            pltpu.VMEM((3, 2, CX, 128), F32),
            pltpu.SemaphoreType.DMA((6,)),
            pltpu.SemaphoreType.DMA((TILES,)),
            pltpu.SemaphoreType.DMA((TILES,)),
            pltpu.SemaphoreType.DMA((TILES,)),
            pltpu.SemaphoreType.DMA((TILES,)),
            pltpu.SemaphoreType.DMA((3, 4)),
            pltpu.SemaphoreType.DMA((3, 4)),
        ],
        compiler_params=pltpu.CompilerParams(
            collective_id=0, has_side_effects=True, vmem_limit_bytes=56 << 20
        ),
    )(gamma, src, dev, blk, coefs, land, state, weights)


PARTS = 4


def finish_kernel(
    gamma,
    state,
    coefs_hbm,
    land_hbm,
    recv,
    section,
    others,
    halo_x_hbm,
    halo_y_hbm,
    new,
    recv_out,
    cells_of,
    around_of,
    start_of,
    done,
    coefs,
    land,
    halo_x,
    halo_y,
    rest,
    csem,
    lsem,
    ssem,
):
    comp = lax.axis_index("comp")
    mix_a, mix_b = mixes(comp)
    depth = CX // PARTS
    common = [
        pltpu.make_async_copy(halo_x_hbm, halo_x, csem.at[0]),
        pltpu.make_async_copy(halo_y_hbm, halo_y, csem.at[1]),
    ]
    loads = []
    for q in range(PARTS):
        rows = pl.ds(q * depth, depth)
        inner = pl.ds(8 + q * depth, depth)
        loads.append(
            [
                pltpu.make_async_copy(section.at[:, rows, :], around_of.at[:, inner, :], lsem.at[q, 0]),
                pltpu.make_async_copy(coefs_hbm.at[:, :, rows, :], coefs.at[:, :, rows, :], lsem.at[q, 1]),
                pltpu.make_async_copy(land_hbm.at[rows, :], land.at[rows, :], lsem.at[q, 2]),
                pltpu.make_async_copy(recv.at[:, rows, :], cells_of.at[:, rows, :], lsem.at[q, 3]),
                pltpu.make_async_copy(state.at[0, 0:CH, rows, :], start_of.at[:, rows, :], lsem.at[q, 4]),
            ]
        )
    kept = pltpu.make_async_copy(others, rest, csem.at[2])
    loads[0][0].start()
    for load in common:
        load.start()
    for load in loads[0][1:]:
        load.start()
    for q in range(1, PARTS):
        for load in loads[q]:
            load.start()
    kept.start()

    for load in common:
        load.wait()
    loads[0][0].wait()
    for f in range(CH):
        around_of[f, 7:8, :] = halo_x[0, f : f + 1, :]
        around_of[f, 8 + CX : 9 + CX, :] = halo_x[1, f : f + 1, :]

    stores = []
    for q in range(PARTS):
        if q + 1 < PARTS:
            loads[q + 1][0].wait()
        for load in loads[q][1:]:
            load.wait()

        def step(i, carry):
            rows = pl.ds(pl.multiple_of(i * 8, 8), 8)
            weight = slopes(rows, coefs, land, comp)
            left, right = halo_y[0, rows, :], halo_y[1, rows, :]
            for f in range(CH):
                cur, prev, nxt = [
                    around_of[f, pl.ds(pl.multiple_of(i * 8 + o, 8), 8), :] for o in (8, 0, 16)
                ]
                rate = stencil(cur, prev, nxt, left[:, f : f + 1], right[:, f : f + 1], weight)
                rate = rate + (gamma[0, f] * weight[5]) * (cells_of[f, rows, :] - cur)
                start = start_of[f, rows, :]
                done[f, rows, :] = mix_a * start + (1.0 - mix_a) * cur + mix_b * rate
            return carry

        rows = pl.ds(q * depth, depth)
        stores.append(
            pltpu.make_async_copy(cells_of.at[:, rows, :], recv_out.at[0, :, rows, :], ssem.at[q, 0])
        )
        stores[-1].start()
        lax.fori_loop(q * (depth // 8), (q + 1) * (depth // 8), step, 0)
        stores.append(
            pltpu.make_async_copy(done.at[:, rows, :], new.at[0, 0:CH, rows, :], ssem.at[q, 1])
        )
        stores[-1].start()
    kept.wait()
    stores.append(pltpu.make_async_copy(rest, new.at[0, CH:NF], csem.at[3]))
    stores[-1].start()
    for store in stores:
        store.wait()


def finish(gamma, state, coefs, land, recv, section, others, halo_x, halo_y):
    hbm = pl.BlockSpec(memory_space=pl.ANY)
    half = pltpu.VMEM((CH, CX, CY), F32)
    return pl.pallas_call(
        finish_kernel,
        out_shape=[
            jax.ShapeDtypeStruct((1, NF, CX, CY), F32),
            jax.ShapeDtypeStruct((1, CH, CX, CY), F32),
        ],
        in_specs=[pl.BlockSpec(memory_space=pltpu.SMEM)] + [hbm] * 8,
        out_specs=[hbm] * 2,
        scratch_shapes=[
            half,
            pltpu.VMEM((CH, CX + 16, CY), F32),
            half,
            half,
            pltpu.VMEM((1, 3, CX, CY), F32),
            pltpu.VMEM((CX, CY), jnp.int32),
            pltpu.VMEM((2, CH, CY), F32),
            pltpu.VMEM((2, CX, 128), F32),
            half,
            pltpu.SemaphoreType.DMA((4,)),
            pltpu.SemaphoreType.DMA((PARTS, 5)),
            pltpu.SemaphoreType.DMA((PARTS, 2)),
        ],
        compiler_params=pltpu.CompilerParams(vmem_limit_bytes=60 << 20),
    )(gamma, state, coefs, land, recv, section, others, halo_x, halo_y)


def body(state, coefs, land_sea, gamma, pair_src, pair_dev, pair_blk, weights):
    recv, section, others, halo_x, halo_y = remap(
        gamma,
        pair_src,
        pair_dev.reshape(1, PAIRS),
        pair_blk,
        coefs,
        land_sea,
        state,
        weights,
    )
    new, recv_out = finish(
        gamma, state, coefs, land_sea, recv, section, others, halo_x, halo_y
    )
    return new, recv_out


def solution(mesh):
    placed = (
        P("comp", None, "tx", "ty"),
        P("comp", None, "tx", "ty"),
        P("tx", "ty"),
        P("comp", None),
        P("comp", ("tx", "ty")),
        P("comp", ("tx", "ty"), None),
        P("comp", ("tx", "ty")),
        P("comp", ("tx", "ty"), None, None),
    )
    return jax.shard_map(
        body,
        mesh=mesh,
        in_specs=placed,
        out_specs=(P("comp", None, "tx", "ty"), P("comp", None, "tx", "ty")),
        check_vma=False,
    )
```

```python
import jax
import jax.numpy as jnp
from jax import lax
from jax.experimental import pallas as pl
from jax.experimental.pallas import tpu as pltpu
from jax.sharding import PartitionSpec as P

MESH = pl.DeviceIdType.MESH
F32 = jnp.float32
BF16 = jnp.bfloat16


TILES = 64
PAIRS = 512
CAP = 16
SLOTS = TILES * CAP
NB = 512
CH = 8
NF = 16
CX = 128
CY = 512


def slopes(rows, coefs, land, comp):
    u = coefs[0, 0, rows, :]
    v = coefs[0, 1, rows, :]
    kappa = coefs[0, 2, rows, :]
    keep = jnp.where(comp == 0, 1.0, land[rows, :].astype(F32))
    return [
        keep * (jnp.maximum(u, 0.0) + kappa),
        keep * (kappa - jnp.minimum(u, 0.0)),
        keep * (jnp.maximum(v, 0.0) + kappa),
        keep * (kappa - jnp.minimum(v, 0.0)),
        -keep * (jnp.abs(u) + jnp.abs(v) + 4.0 * kappa),
        keep,
    ]


def stencil(cur, prev, nxt, left, right, weight):
    sub = lax.broadcasted_iota(jnp.int32, (8, CY), 0)
    lane = lax.broadcasted_iota(jnp.int32, (8, CY), 1)
    up = jnp.where(sub == 0, pltpu.roll(prev, 1, 0), pltpu.roll(cur, 1, 0))
    down = jnp.where(sub == 7, pltpu.roll(nxt, 7, 0), pltpu.roll(cur, 7, 0))
    back = jnp.where(lane == 0, left, pltpu.roll(cur, 1, 1))
    ahead = jnp.where(lane == CY - 1, right, pltpu.roll(cur, CY - 1, 1))
    total = weight[0] * up + weight[1] * down
    total = total + (weight[2] * back + weight[3] * ahead)
    return total + weight[4] * cur


def mixes(comp):
    a = jnp.where(comp == 0, 0.0, 0.5).astype(F32)
    b = jnp.where(comp == 0, 1.0, 0.5).astype(F32)
    return a, b


def remap_kernel(
    gamma,
    src,
    dev,
    blk,
    coefs_hbm,
    land_hbm,
    state,
    weights,
    out,
    section,
    others,
    halo_x,
    halo_y,
    names_of,
    plan,
    table,
    rest,
    cells_of,
    coefs,
    land,
    wbuf,
    surf,
    send,
    recv,
    recv_ids,
    acc,
    sp,
    sq,
    part,
    kc,
    xs,
    xr,
    ys,
    yr,
    lsem,
    ssem,
    rsem,
    isend,
    irecv,
    esend,
    erecv,
):
    comp = lax.axis_index("comp")
    tx = lax.axis_index("tx")
    ty = lax.axis_index("ty")
    h = tx // 4
    x = tx % 4
    y = ty // 2
    core = ty % 2
    sign = 1 - 2 * core

    loads = [
        pltpu.make_async_copy(
            state.at[0, 0:CH], sp.at[0:CH, 8 : 8 + CX, :], lsem.at[0]
        ),
        pltpu.make_async_copy(weights.at[0], wbuf, lsem.at[1]),
        pltpu.make_async_copy(
            state.at[0, CH:NF], sp.at[CH:NF, 8 : 8 + CX, :], lsem.at[2]
        ),
    ]
    loads.append(pltpu.make_async_copy(coefs_hbm, coefs, lsem.at[4]))
    loads.append(pltpu.make_async_copy(land_hbm, land, lsem.at[5]))
    for n in (0, 1, 3, 4, 2):
        loads[n].start()

    def partner(i):
        dh = lax.rem(i, 2)
        dx = lax.rem(lax.div(i, 2), 4)
        dy = lax.rem(lax.div(i, 8) + dx, 4)
        dc = lax.div(i, 32)
        to_x = lax.rem(h + dh, 2) * 4 + lax.rem(x + sign * dx + 4, 4)
        to_y = lax.rem(y + sign * dy + 4, 4) * 2 + lax.rem(core + dc, 2)
        return to_x, to_y

    beside = (
        (comp, lax.rem(tx + 1, 8), ty),
        (comp, lax.rem(tx + 7, 8), ty),
        (comp, tx, lax.rem(ty + 1, 8)),
        (comp, tx, lax.rem(ty + 7, 8)),
    )

    barrier = pltpu.get_barrier_semaphore()

    for to in beside:
        pl.semaphore_signal(barrier, 1, device_id=to, device_id_type=MESH)

    to_xs = [
        lax.rem(h + dh, 2) * 4 + lax.rem(x + sign * dx + 4, 4) for dh in range(2) for dx in range(4)
    ]
    to_ys = [
        lax.rem(y + sign * dy + 4, 4) * 2 + lax.rem(core + dc, 2) for dy in range(4) for dc in range(2)
    ]
    for to_x in to_xs:
        for to_y in to_ys:
            pl.semaphore_signal(barrier, 1, device_id=(1 - comp, to_x, to_y), device_id_type=MESH)

    target = dev[...]
    member = lax.broadcasted_iota(jnp.int32, (TILES, PAIRS), 0) == target
    one_of = jnp.where(member, 1.0, 0.0).astype(BF16)
    before = jnp.where(
        lax.broadcasted_iota(jnp.int32, (PAIRS, PAIRS), 0)
        < lax.broadcasted_iota(jnp.int32, (PAIRS, PAIRS), 1),
        1.0,
        0.0,
    ).astype(BF16)
    counted = jnp.dot(one_of, before, preferred_element_type=F32)
    rank = jnp.sum(jnp.where(member, counted, 0.0), axis=0, keepdims=True)
    at_rank = lax.broadcasted_iota(jnp.int32, (128, PAIRS), 0) % CAP
    at_rank = jnp.where(at_rank.astype(F32) == rank, 1.0, 0.0).astype(BF16)
    number = lax.broadcasted_iota(jnp.int32, (1, PAIRS), 1)
    b = blk[...]
    b = (b // 32) * 32 + (b % 4) * 8 + (b // 4) % 8

    def tabled(value):
        rows = jnp.where(member, value.astype(F32), 0.0).astype(BF16)
        return lax.dot_general(
            rows, at_rank, (((1,), (1,)), ((), ())), preferred_element_type=F32
        )

    def placed(value):
        return 2.0 * tabled(value // 2) + tabled(value % 2)

    table[0] = placed(number).astype(jnp.int32)
    table[1] = placed(src[...]).astype(jnp.int32)
    to_smem = pltpu.make_async_copy(table, plan, lsem.at[3])
    to_smem.start()
    names = placed(b) + float(NB) * (1.0 - tabled(jnp.ones((1, PAIRS), jnp.int32)))
    for d in range(TILES):
        names_of[d] = names[d : d + 1, :]
    loads[0].wait()

    def relay(i, carry):
        for yb in range(4):
            rows = pl.ds(pl.multiple_of(i * 8 + 8, 8), 8)
            tiles = sp[0:CH, rows, yb * 128 : yb * 128 + 128]
            tiles = jnp.swapaxes(tiles, 0, 1)
            for r in range(8):
                surf[i * 32 + r * 4 + yb] = tiles[r]
        return carry

    lax.fori_loop(0, 16, relay, 0)

    def edges(e):
        moves = []
        for n in range(4):
            count = NF if e == 0 else CH
            if n < 2:
                box = (xs.at[e, n, 0:count], xr.at[e, n, 0:count])
            else:
                box = (ys.at[e, n - 2], yr.at[e, n - 2])
            moves.append(
                pltpu.make_async_remote_copy(
                    box[0],
                    box[1],
                    esend.at[e, n],
                    erecv.at[e, n],
                    device_id=beside[n],
                    device_id_type=MESH,
                )
            )
        return moves

    lanes = lax.broadcasted_iota(jnp.int32, (8, 128), 1)

    def pack_columns(e, i, strips):
        first = jnp.zeros((8, 128), F32)
        last = jnp.zeros((8, 128), F32)
        for f, cells in enumerate(strips):
            first = jnp.where(lanes == f, cells[:, 0:1], first)
            last = jnp.where(lanes == f, cells[:, -1:], last)
        rows = pl.ds(pl.multiple_of(i * 8, 8), 8)
        ys[e, 0, rows, :] = last
        ys[e, 1, rows, :] = first

    def settle(e):
        for move in edges(e):
            move.wait_recv()
        for n, (place, end) in enumerate(((tx, 0), (tx, 7))):
            count = NF if e == 0 else CH
            xr[e, n, 0:count] = jnp.where(place == end, 0.0, xr[e, n, 0:count])
        for n, (place, end) in enumerate(((ty, 0), (ty, 7))):
            yr[e, n] = jnp.where(place == end, 0.0, yr[e, n])

    def copies(i):
        to_x, to_y = partner(i)
        to = (1 - comp, to_x, to_y)
        data = pltpu.make_async_remote_copy(
            send.at[i], recv.at[i], ssem.at[i], rsem.at[i], device_id=to, device_id_type=MESH
        )
        names = pltpu.make_async_remote_copy(
            names_of.at[to_x * 8 + to_y],
            recv_ids.at[i],
            isend.at[i],
            irecv.at[i],
            device_id=to,
            device_id_type=MESH,
        )
        return data, names, to_x * 8 + to_y

    to_smem.wait()
    loads[1].wait()
    pl.semaphore_wait(barrier, TILES + 4)

    def produce(i, carry):
        data, names, tile = copies(i)
        names.start()
        zero = jnp.zeros((8, 128), F32)
        for g in range(CAP // 4):
            ws = []
            ps = []
            for j in range(4):
                ws.append(wbuf[jnp.clip(plan[0, tile, g * 4 + j], 0, PAIRS - 1)])
                ps.append(surf[jnp.clip(plan[1, tile, g * 4 + j], 0, NB - 1)])
            lhs = jnp.concatenate(
                [
                    jnp.concatenate([ps[0], zero, ps[2], zero], axis=0),
                    jnp.concatenate([zero, ps[1], zero, ps[3]], axis=0),
                ],
                axis=1,
            ).astype(BF16)
            rhs = jnp.concatenate(
                [
                    jnp.concatenate([ws[0], ws[1]], axis=1),
                    jnp.concatenate([ws[2], ws[3]], axis=1),
                ],
                axis=0,
            )
            both = lax.dot_general(
                lhs, rhs, (((1,), (1,)), ((), ())), preferred_element_type=F32
            )
            parts = [both[0:8, :128], both[8:16, :128], both[16:24, 128:], both[24:32, 128:]]
            for j in range(4):
                send[i, pl.ds(g * 4 + j, 8, stride=CAP), :] = parts[j]
        data.start()
        return carry

    lax.fori_loop(0, 8, produce, 0)
    loads[2].wait()

    def prepare(i, carry):
        rows = pl.ds(pl.multiple_of(i * 8, 8), 8)
        for n, value in enumerate(slopes(rows, coefs, land, comp)):
            kc[n, rows, :] = value
        return carry

    loads[3].wait()
    loads[4].wait()
    lax.fori_loop(0, 16, prepare, 0)

    def pack_state(i, carry):
        rows = pl.ds(pl.multiple_of(i * 8 + 8, 8), 8)
        pack_columns(0, i, [sp[f, rows, :] for f in range(NF)])
        return carry

    lax.fori_loop(0, 16, pack_state, 0)
    for f in range(NF):
        xs[0, 0, f : f + 1, :] = sp[f, 7 + CX : 8 + CX, :]
        xs[0, 1, f : f + 1, :] = sp[f, 8:9, :]

    for move in edges(0):
        move.start()

    lax.fori_loop(8, 40, produce, 0)

    mix_a, mix_b = mixes(comp)
    settle(0)
    for f in range(NF):
        sp[f, 7:8, :] = xr[0, 0, f : f + 1, :]
        sp[f, 8 + CX : 9 + CX, :] = xr[0, 1, f : f + 1, :]

    def around(box, f, i):
        return [box[f, pl.ds(pl.multiple_of(i * 8 + o, 8), 8), :] for o in (8, 0, 16)]

    def first_step(i, carry):
        rows = pl.ds(pl.multiple_of(i * 8, 8), 8)
        weight = [kc[n, rows, :] for n in range(5)]
        keep = kc[5, rows, :]
        left, right = yr[0, 0, rows, :], yr[0, 1, rows, :]
        strips = []
        for f in range(NF):
            cur, prev, nxt = around(sp, f, i)
            rate = stencil(cur, prev, nxt, left[:, f : f + 1], right[:, f : f + 1], weight)
            if f < CH:
                part[f, rows, :] = cur + (rate - (gamma[0, f] * keep) * cur)
            else:
                moved = cur + rate
                sq[f - CH, pl.ds(pl.multiple_of(i * 8 + 8, 8), 8), :] = moved
                strips.append(moved)
        pack_columns(1, i, strips)
        return carry

    lax.fori_loop(0, 16, first_step, 0)
    for f in range(CH):
        xs[1, 0, f : f + 1, :] = sq[f, 7 + CX : 8 + CX, :]
        xs[1, 1, f : f + 1, :] = sq[f, 8:9, :]
    for move in edges(1):
        move.start()
    lax.fori_loop(40, TILES, produce, 0)
    settle(1)
    for f in range(CH):
        sq[f, 7:8, :] = xr[1, 0, f : f + 1, :]
        sq[f, 8 + CX : 9 + CX, :] = xr[1, 1, f : f + 1, :]

    def second_step(i, carry):
        rows = pl.ds(pl.multiple_of(i * 8, 8), 8)
        weight = [kc[n, rows, :] for n in range(5)]
        left, right = yr[1, 0, rows, :], yr[1, 1, rows, :]
        for f in range(CH):
            cur, prev, nxt = around(sq, f, i)
            rate = stencil(cur, prev, nxt, left[:, f : f + 1], right[:, f : f + 1], weight)
            start = sp[f + CH, pl.ds(pl.multiple_of(i * 8 + 8, 8), 8), :]
            rest[f, rows, :] = mix_a * start + (1.0 - mix_a) * cur + mix_b * rate
        return carry

    lax.fori_loop(0, 16, second_step, 0)
    stores = [pltpu.make_async_copy(rest, others, lsem.at[0])]
    stores[0].start()

    def arrive(i, carry):
        data, names, _ = copies(i)
        names.wait_recv()
        data.wait_recv()
        return carry

    seg = lax.broadcasted_iota(jnp.int32, (8, 128), 1) // CAP == lax.broadcasted_iota(
        jnp.int32, (8, 128), 0
    )
    for q in range(4):
        lax.fori_loop(16 * q, 16 * q + 16, arrive, 0)
        names = []
        for half in range(2):
            first = q * 16 + half * 8
            rows = jnp.concatenate([recv_ids[first + j] for j in range(8)], axis=0)
            names.append(jnp.sum(jnp.where(seg, rows, 0.0), axis=0, keepdims=True))
        wanted = jnp.concatenate(names, axis=1)
        blocks = lax.broadcasted_iota(jnp.int32, (NB, 256), 0).astype(F32)
        select = jnp.where(blocks == wanted, 1.0, 0.0).astype(BF16)
        for c in range(0, CH, 2):
            cols = []
            for cc in (c, c + 1):
                cols.append(
                    jnp.concatenate(
                        [recv[q * 16 + j, cc * CAP : cc * CAP + CAP, :] for j in range(16)], axis=0
                    )
                )
            terms = jnp.concatenate(cols, axis=1)
            high = terms.astype(BF16)
            low = (terms - high.astype(F32)).astype(BF16)
            total = jnp.dot(select, high, preferred_element_type=F32)
            total = total + jnp.dot(select, low, preferred_element_type=F32)
            for cc in range(2):
                piece = total[:, cc * 128 : cc * 128 + 128]
                if q == 0:
                    acc[c + cc] = piece
                else:
                    acc[c + cc] += piece

    def couple(i, carry):
        rows = pl.ds(pl.multiple_of(i * 8, 8), 8)
        keep = kc[5, rows, :]
        strips = []
        for f in range(CH):
            cells = jnp.concatenate(
                [acc[f, pl.ds(pl.multiple_of(i * 32 + yb * 8, 8), 8), :] for yb in range(4)],
                axis=1,
            )
            cells_of[f, rows, :] = cells
            moved = part[f, rows, :] + (gamma[0, f] * keep) * cells
            sq[f, pl.ds(pl.multiple_of(i * 8 + 8, 8), 8), :] = moved
            strips.append(moved)
        pack_columns(2, i, strips)
        return carry

    lax.fori_loop(0, 16, couple, 0)
    for f in range(CH):
        xs[2, 0, f : f + 1, :] = sq[f, 7 + CX : 8 + CX, :]
        xs[2, 1, f : f + 1, :] = sq[f, 8:9, :]
    for move in edges(2):
        move.start()
    stores.append(
        pltpu.make_async_copy(sq.at[:, 8 : 8 + CX, :], section, lsem.at[2])
    )
    stores.append(pltpu.make_async_copy(cells_of, out, lsem.at[1]))
    for store in stores[1:]:
        store.start()

    def sent(i, carry):
        data, names, _ = copies(i)
        names.wait_send()
        data.wait_send()
        return carry

    settle(2)
    for copy in (
        pltpu.make_async_copy(xr.at[2, :, 0:CH, :], halo_x, lsem.at[3]),
        pltpu.make_async_copy(yr.at[2], halo_y, lsem.at[4]),
    ):
        copy.start()
        stores.append(copy)
    lax.fori_loop(0, TILES, sent, 0)
    for e in range(3):
        for move in edges(e):
            move.wait_send()
    for store in stores:
        store.wait()


def remap(gamma, src, dev, blk, coefs, land, state, weights):
    smem = pl.BlockSpec(memory_space=pltpu.SMEM)
    vmem = pl.BlockSpec(memory_space=pltpu.VMEM)
    hbm = pl.BlockSpec(memory_space=pl.ANY)
    half = jax.ShapeDtypeStruct((CH, CX, CY), F32)
    return pl.pallas_call(
        remap_kernel,
        out_shape=[
            half,
            half,
            half,
            jax.ShapeDtypeStruct((2, CH, CY), F32),
            jax.ShapeDtypeStruct((2, CX, 128), F32),
        ],
        in_specs=[smem, vmem, vmem, vmem, hbm, hbm, hbm, hbm],
        out_specs=[hbm] * 5,
        scratch_shapes=[
            pltpu.VMEM((TILES, 1, 128), F32),
            pltpu.SMEM((2, TILES, 128), jnp.int32),
            pltpu.VMEM((2, TILES, 128), jnp.int32),
            pltpu.VMEM((CH, CX, CY), F32),
            pltpu.VMEM((CH, CX, CY), F32),
            pltpu.VMEM((1, 3, CX, CY), F32),
            pltpu.VMEM((CX, CY), jnp.int32),
            pltpu.VMEM((PAIRS, 128, 128), BF16),
            pltpu.VMEM((NB, CH, 128), F32),
            pltpu.VMEM((TILES, CH * CAP, 128), F32),
            pltpu.VMEM((TILES, CH * CAP, 128), F32),
            pltpu.VMEM((TILES, 1, 128), F32),
            pltpu.VMEM((CH, NB, 128), F32),
            pltpu.VMEM((NF, CX + 16, CY), F32),
            pltpu.VMEM((CH, CX + 16, CY), F32),
            pltpu.VMEM((CH, CX, CY), F32),
            pltpu.VMEM((6, CX, CY), F32),
            pltpu.VMEM((3, 2, NF, CY), F32),
            pltpu.VMEM((3, 2, NF, CY), F32),
            pltpu.VMEM((3, 2, CX, 128), F32),
            pltpu.VMEM((3, 2, CX, 128), F32),
            pltpu.SemaphoreType.DMA((6,)),
            pltpu.SemaphoreType.DMA((TILES,)),
            pltpu.SemaphoreType.DMA((TILES,)),
            pltpu.SemaphoreType.DMA((TILES,)),
            pltpu.SemaphoreType.DMA((TILES,)),
            pltpu.SemaphoreType.DMA((3, 4)),
            pltpu.SemaphoreType.DMA((3, 4)),
        ],
        compiler_params=pltpu.CompilerParams(
            collective_id=0, has_side_effects=True, vmem_limit_bytes=56 << 20
        ),
    )(gamma, src, dev, blk, coefs, land, state, weights)


PARTS = 2


def finish_kernel(
    gamma,
    state,
    coefs_hbm,
    land_hbm,
    recv,
    section,
    others,
    halo_x_hbm,
    halo_y_hbm,
    new,
    recv_out,
    cells_of,
    around_of,
    start_of,
    done,
    coefs,
    land,
    halo_x,
    halo_y,
    rest,
    csem,
    lsem,
    ssem,
):
    comp = lax.axis_index("comp")
    mix_a, mix_b = mixes(comp)
    depth = CX // PARTS
    common = [
        pltpu.make_async_copy(halo_x_hbm, halo_x, csem.at[0]),
        pltpu.make_async_copy(halo_y_hbm, halo_y, csem.at[1]),
    ]
    loads = []
    for q in range(PARTS):
        rows = pl.ds(q * depth, depth)
        inner = pl.ds(8 + q * depth, depth)
        loads.append(
            [
                pltpu.make_async_copy(section.at[:, rows, :], around_of.at[:, inner, :], lsem.at[q, 0]),
                pltpu.make_async_copy(coefs_hbm.at[:, :, rows, :], coefs.at[:, :, rows, :], lsem.at[q, 1]),
                pltpu.make_async_copy(land_hbm.at[rows, :], land.at[rows, :], lsem.at[q, 2]),
                pltpu.make_async_copy(recv.at[:, rows, :], cells_of.at[:, rows, :], lsem.at[q, 3]),
                pltpu.make_async_copy(state.at[0, 0:CH, rows, :], start_of.at[:, rows, :], lsem.at[q, 4]),
            ]
        )
    kept = pltpu.make_async_copy(others, rest, csem.at[2])
    loads[0][0].start()
    for load in common:
        load.start()
    for load in loads[0][1:]:
        load.start()
    for q in range(1, PARTS):
        for load in loads[q]:
            load.start()
    kept.start()

    for load in common:
        load.wait()
    loads[0][0].wait()
    for f in range(CH):
        around_of[f, 7:8, :] = halo_x[0, f : f + 1, :]
        around_of[f, 8 + CX : 9 + CX, :] = halo_x[1, f : f + 1, :]

    stores = []
    for q in range(PARTS):
        if q + 1 < PARTS:
            loads[q + 1][0].wait()
        for load in loads[q][1:]:
            load.wait()

        def step(i, carry):
            rows = pl.ds(pl.multiple_of(i * 8, 8), 8)
            weight = slopes(rows, coefs, land, comp)
            left, right = halo_y[0, rows, :], halo_y[1, rows, :]
            for f in range(CH):
                cur, prev, nxt = [
                    around_of[f, pl.ds(pl.multiple_of(i * 8 + o, 8), 8), :] for o in (8, 0, 16)
                ]
                rate = stencil(cur, prev, nxt, left[:, f : f + 1], right[:, f : f + 1], weight)
                rate = rate + (gamma[0, f] * weight[5]) * (cells_of[f, rows, :] - cur)
                start = start_of[f, rows, :]
                done[f, rows, :] = mix_a * start + (1.0 - mix_a) * cur + mix_b * rate
            return carry

        rows = pl.ds(q * depth, depth)
        stores.append(
            pltpu.make_async_copy(cells_of.at[:, rows, :], recv_out.at[0, :, rows, :], ssem.at[q, 0])
        )
        stores[-1].start()
        lax.fori_loop(q * (depth // 8), (q + 1) * (depth // 8), step, 0)
        stores.append(
            pltpu.make_async_copy(done.at[:, rows, :], new.at[0, 0:CH, rows, :], ssem.at[q, 1])
        )
        stores[-1].start()
    kept.wait()
    stores.append(pltpu.make_async_copy(rest, new.at[0, CH:NF], csem.at[3]))
    stores[-1].start()
    for store in stores:
        store.wait()


def finish(gamma, state, coefs, land, recv, section, others, halo_x, halo_y):
    hbm = pl.BlockSpec(memory_space=pl.ANY)
    half = pltpu.VMEM((CH, CX, CY), F32)
    return pl.pallas_call(
        finish_kernel,
        out_shape=[
            jax.ShapeDtypeStruct((1, NF, CX, CY), F32),
            jax.ShapeDtypeStruct((1, CH, CX, CY), F32),
        ],
        in_specs=[pl.BlockSpec(memory_space=pltpu.SMEM)] + [hbm] * 8,
        out_specs=[hbm] * 2,
        scratch_shapes=[
            half,
            pltpu.VMEM((CH, CX + 16, CY), F32),
            half,
            half,
            pltpu.VMEM((1, 3, CX, CY), F32),
            pltpu.VMEM((CX, CY), jnp.int32),
            pltpu.VMEM((2, CH, CY), F32),
            pltpu.VMEM((2, CX, 128), F32),
            half,
            pltpu.SemaphoreType.DMA((4,)),
            pltpu.SemaphoreType.DMA((PARTS, 5)),
            pltpu.SemaphoreType.DMA((PARTS, 2)),
        ],
        compiler_params=pltpu.CompilerParams(vmem_limit_bytes=60 << 20),
    )(gamma, state, coefs, land, recv, section, others, halo_x, halo_y)


def body(state, coefs, land_sea, gamma, pair_src, pair_dev, pair_blk, weights):
    recv, section, others, halo_x, halo_y = remap(
        gamma,
        pair_src,
        pair_dev.reshape(1, PAIRS),
        pair_blk,
        coefs,
        land_sea,
        state,
        weights,
    )
    new, recv_out = finish(
        gamma, state, coefs, land_sea, recv, section, others, halo_x, halo_y
    )
    return new, recv_out


def solution(mesh):
    placed = (
        P("comp", None, "tx", "ty"),
        P("comp", None, "tx", "ty"),
        P("tx", "ty"),
        P("comp", None),
        P("comp", ("tx", "ty")),
        P("comp", ("tx", "ty"), None),
        P("comp", ("tx", "ty")),
        P("comp", ("tx", "ty"), None, None),
    )
    return jax.shard_map(
        body,
        mesh=mesh,
        in_specs=placed,
        out_specs=(P("comp", None, "tx", "ty"), P("comp", None, "tx", "ty")),
        check_vma=False,
    )
```
